32 devices in a mesh: gy: 8 (over z, y), gz: 4 (over x, core).
Axes of the slice: x: 2, y: 2, z: 4, core: 2. Of those that a mesh axis runs over, the one named last changes fastest.
Arguments:
- flow_state: bfloat16 [4, 128, 64, 512], P(None, 'gz', 'gy'), may hold values from -4 to 4
- metric: float32 [3, 3], replicated, may hold values from -0.3 to 1.5, as said below
- deformation_matrix: float32 [3, 3], replicated, may hold values from -0.5 to 0.5
Outputs:
- solenoidal_motion: float32 [3, 128, 64, 512], P(None, 'gz', 'gy')
- heat_content_next: float32 [128, 64, 512], P('gz', 'gy')
The draws below stay inside these ranges and needn't reach their ends.
Inputs may be any that keep to these rules, and one draw needn't show every extreme that they name: `metric`: diagonal entries lie between 1 and 1.5, off-diagonal entries have magnitude at most 0.3.
All inputs are finite; a program needn't handle non-finite values.
Results may differ from the reference program's by a relative error of at most 0.0003.
Values may be sent and summed in bfloat16 or wider, within the bound.
A program may use at most 128 MiB of HBM per device.

```python
import math
import jax
import jax.numpy as jnp

NX = 512
NY = 64
NZ = 128


def draw_flow_state(key, part):
    key = jax.random.fold_in(key, 11)
    extent = (4, NZ, NY, NX)
    values = jnp.clip(jax.random.normal(key, extent, jnp.float32), -4.0, 4.0)
    return values.astype(jnp.bfloat16)


def draw_metric(key, part):
    key = jax.random.fold_in(key, 23)
    leading, second = jax.random.split(key)
    diagonal_top = 1.5
    diagonal_values = jax.random.uniform(leading, (3, 3), jnp.float32, 1.0, diagonal_top)
    outside_values = jax.random.uniform(second, (3, 3), jnp.float32, -0.3, 0.3)
    rows_iota = jnp.arange(3, dtype=jnp.int32)[:, None]
    cols_iota = jnp.arange(3, dtype=jnp.int32)[None, :]
    return jnp.where(rows_iota == cols_iota, diagonal_values, outside_values)


def setup_inputs(seed: int = 0) -> dict:
    seeds = jax.random.split(jax.random.key(seed), 4)
    flow_state = draw_flow_state(jax.random.fold_in(seeds[3], 71), 0)
    metric = draw_metric(jax.random.fold_in(seeds[3], 71), 0)
    deformation_matrix = jnp.clip(jax.random.uniform(seeds[2], (3, 3), jnp.float32, -0.5, 0.5), -0.5, 0.5)
    return dict(flow_state=flow_state, metric=metric, deformation_matrix=deformation_matrix)


substep_width = 0.4
stratification_squared = 1.0


def difference_periodic(forcing_term, along):
    def moved(offset):
        return jnp.roll(forcing_term, -offset, axis=along)
    return (45.0 * (moved(1) - moved(-1)) - 9.0 * (moved(2) - moved(-2)) + (moved(3) - moved(-3))) / 60.0


def wavenumber(modes, length):
    def wave(multiple):
        return jnp.sin((2.0 * math.pi / length) * ((multiple * modes) % length).astype(jnp.float32))
    return 1.5 * wave(1) - 0.3 * wave(2) + wave(3) / 30.0


def reference(flow_state, metric, deformation_matrix):
    state_collection = flow_state.astype(jnp.float32)
    current_speeds = [state_collection[0], state_collection[1], state_collection[2]]
    heat_content = state_collection[3]
    contra = [metric[0, direction] * current_speeds[0] + metric[1, direction] * current_speeds[1] + metric[2, direction] * current_speeds[2] for direction in range(3)]

    def background_stream(forcing_term):
        return contra[0] * difference_periodic(forcing_term, 2) + contra[1] * difference_periodic(forcing_term, 1) + contra[2] * difference_periodic(forcing_term, 0)

    provisional = []
    for vector_entry in range(3):
        evolution_change = -background_stream(current_speeds[vector_entry]) - (deformation_matrix[vector_entry, 0] * current_speeds[0] + deformation_matrix[vector_entry, 1] * current_speeds[1] + deformation_matrix[vector_entry, 2] * current_speeds[2])
        if vector_entry == 2:
            evolution_change = evolution_change + heat_content
        provisional.append(current_speeds[vector_entry] + substep_width * evolution_change)
    heat_content_next = heat_content + substep_width * (-background_stream(heat_content) - stratification_squared * current_speeds[2])
    flow_compressibility = jnp.zeros_like(heat_content)
    for vector_entry in range(3):
        flow_compressibility = flow_compressibility + metric[vector_entry, 0] * difference_periodic(provisional[vector_entry], 2) + metric[vector_entry, 1] * difference_periodic(provisional[vector_entry], 1) + metric[vector_entry, 2] * difference_periodic(provisional[vector_entry], 0)
    spectrum = jnp.fft.fftn(flow_compressibility)
    modes_z = jnp.arange(NZ, dtype=jnp.int32)[:, None, None]
    modes_y = jnp.arange(NY, dtype=jnp.int32)[None, :, None]
    modes_x = jnp.arange(NX, dtype=jnp.int32)[None, None, :]
    waves = [wavenumber(modes_x, NX), wavenumber(modes_y, NY), wavenumber(modes_z, NZ)]
    symbol = jnp.zeros((NZ, NY, NX), jnp.float32)
    for vector_entry in range(3):
        mixed = metric[vector_entry, 0] * waves[0] + metric[vector_entry, 1] * waves[1] + metric[vector_entry, 2] * waves[2]
        symbol = symbol + mixed * mixed
    edge = ((2 * modes_x) % NX == 0) & ((2 * modes_y) % NY == 0) & ((2 * modes_z) % NZ == 0)
    pressure_hat = jnp.where(edge, 0.0, -spectrum / jnp.where(edge, 1.0, symbol))
    pressure = jnp.real(jnp.fft.ifftn(pressure_hat))
    push_x = difference_periodic(pressure, 2)
    push_y = difference_periodic(pressure, 1)
    push_z = difference_periodic(pressure, 0)
    solenoidal_motion = jnp.stack([provisional[vector_entry] - (metric[vector_entry, 0] * push_x + metric[vector_entry, 1] * push_y + metric[vector_entry, 2] * push_z) for vector_entry in range(3)])
    return solenoidal_motion, heat_content_next
```

```python
import numpy as np

import jax
import jax.numpy as jnp
from jax import lax
from jax.sharding import PartitionSpec as P

substep_width = 0.4
high = lax.Precision.HIGH


def halos(block, axis, dim, width):
    count = lax.axis_size(axis)
    forward = [(i, (i + 1) % count) for i in range(count)]
    backward = [((i + 1) % count, i) for i in range(count)]
    low = lax.ppermute(
        lax.slice_in_dim(block, block.shape[dim] - width, None, axis=dim), axis, forward
    )
    high_side = lax.ppermute(lax.slice_in_dim(block, 0, width, axis=dim), axis, backward)
    return jnp.concatenate([low, block, high_side], axis=dim)


def stencil(moved):
    return (
        45.0 * (moved(1) - moved(-1)) - 9.0 * (moved(2) - moved(-2)) + (moved(3) - moved(-3))
    ) / 60.0


def diff_roll(f, along):
    return stencil(lambda offset: jnp.roll(f, -offset, axis=along))


def diff_pad(padded, along):
    extent = padded.shape[along] - 6
    return stencil(lambda o: lax.slice_in_dim(padded, 3 + o, 3 + o + extent, axis=along))


def x_tables(length):
    half = length // 2
    k = np.arange(half)[:, None]
    x = np.arange(length)[None, :]
    angle = 2.0 * np.pi * ((k * x) % length) / length
    c, s = np.cos(angle), -np.sin(angle)
    s[0] = np.where(np.arange(length) % 2 == 0, 1.0, -1.0)
    weight = np.where(np.arange(half) == 0, 1.0, 2.0)[:, None]
    return c, s, weight


def by_owner(re, im, owners):
    half, length = re.shape
    m = half // owners
    return np.concatenate(
        [re.reshape(owners, m, length), im.reshape(owners, m, length)], axis=1
    ).reshape(2 * half, length)


def wave(m, length):
    a = 2.0 * np.pi * m / length
    value = 1.5 * np.sin(a) - 0.3 * np.sin(2 * a) + np.sin(3 * a) / 30.0
    return np.where((2 * m) % length == 0, 0.0, value)


def plane_tables(gy, gz, ey, ez):
    ly, lz = gy * ey, gz * ez
    b = np.repeat(np.arange(ez), ey)
    e = np.tile(np.arange(ey), ez)
    s = np.repeat(np.arange(gy), gz)[:, None]
    q = np.tile(np.arange(gz), gy)[:, None]
    twist = -2.0 * np.pi * (b * q / lz + e * s / ly)
    kron = -2.0 * np.pi * (np.outer(b, b) / ez + np.outer(e, e) / ey)
    my = gy * e[None, :] + s
    mz = gz * b[None, :] + q
    block = -2.0 * np.pi * (
        np.outer(s, s) / gy + np.outer(q, q) / gz
    )
    edge = ((2 * my) % ly == 0) & ((2 * mz) % lz == 0)
    return twist, kron, block, wave(my, ly), wave(mz, lz), edge


def f32(a):
    return jnp.asarray(np.asarray(a, np.float32))


def shards(flow_state, metric, deformation):
    gy, gz = lax.axis_size("gy"), lax.axis_size("gz")
    owners = gy * gz
    _, ez, ey, lx = flow_state.shape
    cells = ez * ey
    me = lax.axis_index("gy") * gz + lax.axis_index("gz")

    state = flow_state.astype(jnp.float32)
    y_pad = halos(flow_state, "gy", 2, 3).astype(jnp.float32)
    z_pad = halos(flow_state, "gz", 1, 3).astype(jnp.float32)
    gx, gyy, gzz = diff_roll(state, 3), diff_pad(y_pad, 2), diff_pad(z_pad, 1)
    speeds, heat = state[:3], state[3]
    contra = [sum(metric[k, j] * speeds[k] for k in range(3)) for j in range(3)]
    carried = contra[0] * gx + contra[1] * gyy + contra[2] * gzz
    prov = []
    for c in range(3):
        change = -carried[c] - sum(deformation[c, l] * speeds[l] for l in range(3))
        if c == 2:
            change = change + heat
        prov.append(speeds[c] + substep_width * change)
    heat_next = heat + substep_width * (-carried[3] - speeds[2])

    flux = [sum(metric[c, j] * prov[c] for c in range(3)) for j in range(3)]
    div = (
        diff_roll(flux[0], 2)
        + diff_pad(halos(flux[1], "gy", 1, 3), 1)
        + diff_pad(halos(flux[2], "gz", 0, 3), 0)
    )

    cos_x, sin_x, weight = x_tables(lx)
    ahead = f32(by_owner(cos_x, sin_x, owners))
    back = f32(by_owner(cos_x * weight, sin_x * weight, owners))
    m = lx // 2 // owners
    spec = jnp.einsum("kx,rx->kr", ahead, div.reshape(cells, lx), precision=high)
    spec = lax.all_to_all(
        spec.reshape(owners, 2 * m, cells), ("gy", "gz"), split_axis=0, concat_axis=0, tiled=True
    )
    twist, kron, block, ky, kz, edge = plane_tables(gy, gz, ey, ez)
    tr, ti = f32(np.cos(twist))[:, None], f32(np.sin(twist))[:, None]
    wr, wi = f32(np.cos(kron)), f32(np.sin(kron))
    br, bi = f32(np.cos(block)), f32(np.sin(block))

    def ein(form, a, b):
        return jnp.einsum(form, a, b, precision=high)

    re, im = spec[:, :m], spec[:, m:]
    re, im = (
        ein("ts,smr->tmr", br, re) - ein("ts,smr->tmr", bi, im),
        ein("ts,smr->tmr", br, im) + ein("ts,smr->tmr", bi, re),
    )
    re, im = re * tr - im * ti, re * ti + im * tr
    re, im = (
        ein("tmr,rp->tmp", re, wr) - ein("tmr,rp->tmp", im, wi),
        ein("tmr,rp->tmp", im, wr) + ein("tmr,rp->tmp", re, wi),
    )
    modes = me * m + jnp.arange(m)
    kx = jnp.take(f32(wave(np.arange(lx // 2), lx)), modes)[None, :, None]
    ky, kz = f32(ky)[:, None], f32(kz)[:, None]
    symbol = sum((metric[c, 0] * kx + metric[c, 1] * ky + metric[c, 2] * kz) ** 2 for c in range(3))
    at_edge = jnp.asarray(edge)[:, None] & (modes == 0)[None, :, None]
    total = float(lx * ey * gy * ez * gz)
    factor = jnp.where(at_edge, 0.0, -1.0 / (jnp.where(at_edge, 1.0, symbol) * total))
    re, im = re * factor, im * factor
    re, im = (
        ein("tmr,rp->tmp", re, wr) + ein("tmr,rp->tmp", im, wi),
        ein("tmr,rp->tmp", im, wr) - ein("tmr,rp->tmp", re, wi),
    )
    re, im = re * tr + im * ti, im * tr - re * ti
    re, im = (
        ein("ts,smr->tmr", br, re) + ein("ts,smr->tmr", bi, im),
        ein("ts,smr->tmr", br, im) - ein("ts,smr->tmr", bi, re),
    )
    spec = lax.all_to_all(
        jnp.concatenate([re, im], axis=1), ("gy", "gz"), split_axis=0, concat_axis=0, tiled=True
    )
    pressure = jnp.einsum("kr,kx->rx", spec.reshape(lx, cells), back, precision=high)
    pressure = pressure.reshape(ez, ey, lx)
    push = [
        diff_roll(pressure, 2),
        diff_pad(halos(pressure, "gy", 1, 3), 1),
        diff_pad(halos(pressure, "gz", 0, 3), 0),
    ]
    motion = jnp.stack([prov[c] - sum(metric[c, j] * push[j] for j in range(3)) for c in range(3)])
    return motion, heat_next


def solution(mesh):
    placed = (P(None, "gz", "gy", None), P(), P())
    return jax.shard_map(
        shards,
        mesh=mesh,
        in_specs=placed,
        out_specs=(P(None, "gz", "gy", None), P("gz", "gy", None)),
        check_vma=False,
    )
```

```python
import numpy as np

import jax
import jax.numpy as jnp
from jax import lax
from jax.experimental import pallas as pl
from jax.experimental.pallas import tpu as pltpu
from jax.sharding import PartitionSpec as P

substep_width = 0.4
mesh_ids = pl.DeviceIdType.MESH
coefs = {1: 45.0, 2: -9.0, 3: 1.0, -1: -45.0, -2: 9.0, -3: -1.0}


def x_tables(length):
    half = length // 2
    k = np.arange(half)[:, None]
    x = np.arange(length)[None, :]
    angle = 2.0 * np.pi * ((k * x) % length) / length
    c, s = np.cos(angle), -np.sin(angle)
    s[0] = np.where(np.arange(length) % 2 == 0, 1.0, -1.0)
    weight = np.where(np.arange(half) == 0, 1.0, 2.0)[:, None]
    return c, s, weight


def by_owner(re, im, owners):
    half, length = re.shape
    m = half // owners
    return np.concatenate(
        [re.reshape(owners, m, length), im.reshape(owners, m, length)], axis=1
    ).reshape(2 * half, length)


def wave(m, length):
    a = 2.0 * np.pi * m / length
    value = 1.5 * np.sin(a) - 0.3 * np.sin(2 * a) + np.sin(3 * a) / 30.0
    return np.where((2 * m) % length == 0, 0.0, value)


def plane_tables(gy, gz, ey, ez):
    ly, lz = gy * ey, gz * ez
    b = np.repeat(np.arange(ez), ey)
    e = np.tile(np.arange(ey), ez)
    s = np.repeat(np.arange(gy), gz)[:, None]
    q = np.tile(np.arange(gz), gy)[:, None]
    twist = -2.0 * np.pi * (b * q / lz + e * s / ly)
    kron = -2.0 * np.pi * (np.outer(b, b) / ez + np.outer(e, e) / ey)
    my = gy * e[None, :] + s
    mz = gz * b[None, :] + q
    block = -2.0 * np.pi * (
        np.outer(s, s) / gy + np.outer(q, q) / gz
    )
    edge = ((2 * my) % ly == 0) & ((2 * mz) % lz == 0)
    return twist, kron, block, wave(my, ly), wave(mz, lz), edge


def stencil_tables(ez, ey, lx):
    cells = ez * ey
    own = np.zeros((2 * cells, cells))
    beside = np.zeros((2 * cells, 6 * ez + 8 * ey))
    pick = np.zeros((6 * ez, cells))
    for z in range(ez):
        for y in range(ey):
            r = z * ey + y
            for o, w in coefs.items():
                t = y + o
                if 0 <= t < ey:
                    own[r, z * ey + t] += w
                elif t < 0:
                    beside[r, (t + 3) * ez + z] += w
                else:
                    beside[r, (3 + t - ey) * ez + z] += w
                t = z + o
                if 0 <= t < ez:
                    own[cells + r, t * ey + y] += w
                elif t < 0:
                    beside[cells + r, 6 * ez + (t + 4) * ey + y] += w
                else:
                    beside[cells + r, 6 * ez + 4 * ey + (t - ez) * ey + y] += w
        for j in range(3):
            pick[j * ez + z, z * ey + ey - 3 + j] = 1.0
            pick[(3 + j) * ez + z, z * ey + j] = 1.0
    along_x = np.zeros((lx, lx))
    for o, w in coefs.items():
        x = np.arange(lx)
        along_x[(x + o) % lx, x] += w
    return own, beside, pick, along_x


def halves(a):
    a = np.asarray(a, np.float32)
    top = a.astype(jnp.bfloat16)
    return [top, (a - top.astype(np.float32)).astype(jnp.bfloat16)]


def split(x, pieces=2):
    out = []
    for _ in range(pieces):
        top = x.astype(jnp.bfloat16)
        out.append(top)
        x = x - top.astype(jnp.float32)
    return out


def dot(a, b, ca=1, cb=0):
    return lax.dot_general(a, b, (((ca,), (cb,)), ((), ())), preferred_element_type=jnp.float32)


def dot3(a, b, ca=1, cb=0):
    return dot(a[0], b[0], ca, cb) + dot(a[0], b[1], ca, cb) + dot(a[1], b[0], ca, cb)


def kernel(
    sizes, metric, deform, state, own, beside, beside_sum, pick, along_x, big_hbm, plane_hbm,
    motion, heat_next,
    big, plane, edge_state, halo_state, grad, grad_x, prov, flux, edge_f, halo_f, div,
    edge_p, halo_p, press, line, there, here, there2, here2, factor,
    load_sem, s_send, s_recv, f_send, f_recv, p_send, p_recv, a_send, a_recv, b_send, b_recv,
):
    gy, gz, ez, ey, lx = sizes
    owners = gy * gz
    cells = ez * ey
    rows2 = lx // owners
    m = rows2 // 2
    ye, ze = 3 * ez, 4 * ey
    iy, iz = lax.axis_index("gy"), lax.axis_index("gz")
    me = iy * gz + iz
    up_y = (lax.rem(iy + 1, gy), iz)
    down_y = (lax.rem(iy + gy - 1, gy), iz)
    up_z = (iy, lax.rem(iz + 1, gz))
    down_z = (iy, lax.rem(iz + gz - 1, gz))

    load_big = pltpu.make_async_copy(big_hbm, big, load_sem.at[0])
    load_plane = pltpu.make_async_copy(plane_hbm, plane, load_sem.at[1])
    load_big.start()
    load_plane.start()

    barrier = pltpu.get_barrier_semaphore()

    def greet(i, carry):
        other = lax.rem(me + i, owners)
        pl.semaphore_signal(
            barrier, inc=1, device_id=(other // gz, lax.rem(other, gz)), device_id_type=mesh_ids
        )
        return carry

    lax.fori_loop(1, owners, greet, 0)

    for c in range(4):
        picked = dot(pick[...], state[c]).astype(jnp.bfloat16)
        edge_state[0, c] = picked[:ye]
        edge_state[1, c] = picked[ye:]
    pl.semaphore_wait(barrier, owners - 1)

    def send(src, dst, send_sem, recv_sem, to):
        copy = pltpu.make_async_remote_copy(
            src_ref=src, dst_ref=dst, send_sem=send_sem, recv_sem=recv_sem,
            device_id=to, device_id_type=mesh_ids,
        )
        copy.start()
        return copy

    halo_copies = [
        send(edge_state.at[0], halo_state.at[:, 0:ye], s_send.at[0], s_recv.at[0], up_y),
        send(edge_state.at[1], halo_state.at[:, ye : 2 * ye], s_send.at[1], s_recv.at[1], down_y),
        send(
            state.at[:, cells - ze : cells], halo_state.at[:, 2 * ye : 2 * ye + ze],
            s_send.at[2], s_recv.at[2], up_z,
        ),
        send(
            state.at[:, 0:ze], halo_state.at[:, 2 * ye + ze : 2 * ye + 2 * ze],
            s_send.at[3], s_recv.at[3], down_z,
        ),
    ]
    for c in range(4):
        grad[c] = dot(own[...], state[c])
        grad_x[c] = dot(state[c], along_x[...])
    for copy in halo_copies:
        copy.wait()
    for c in range(4):
        grad[c] += dot(beside[...], halo_state[c])

    sixtieth = 1.0 / 60.0

    def advance(i, carry):
        rows = pl.ds(pl.multiple_of(i * 16, 16), 16)
        rows_z = pl.ds(pl.multiple_of(cells + i * 16, 16), 16)
        f = [state[c, rows, :].astype(jnp.float32) for c in range(4)]
        contra = [
            (metric[0, j] * f[0] + metric[1, j] * f[1] + metric[2, j] * f[2]) * sixtieth
            for j in range(3)
        ]
        carried = [
            contra[0] * grad_x[c, rows, :]
            + contra[1] * grad[c, rows, :]
            + contra[2] * grad[c, rows_z, :]
            for c in range(4)
        ]
        new = []
        for c in range(3):
            change = -carried[c] - (
                deform[c, 0] * f[0] + deform[c, 1] * f[1] + deform[c, 2] * f[2]
            )
            if c == 2:
                change = change + f[3]
            new.append(f[c] + substep_width * change)
            prov[c, rows, :] = new[c]
        heat_next[rows, :] = f[3] + substep_width * (-carried[3] - f[2])
        for j in range(3):
            flux[j, rows, :] = metric[0, j] * new[0] + metric[1, j] * new[1] + metric[2, j] * new[2]
        return carry

    lax.fori_loop(0, cells // 16, advance, 0)

    f1 = split(flux[1])
    f2 = split(flux[2])
    edge_f[...] = dot(pick[...], f1[0]) + dot(pick[...], f1[1])
    halo_copies = [
        send(edge_f.at[0:ye], halo_f.at[0:ye], f_send.at[0], f_recv.at[0], up_y),
        send(edge_f.at[ye : 2 * ye], halo_f.at[ye : 2 * ye], f_send.at[1], f_recv.at[1], down_y),
        send(
            flux.at[2, cells - ze : cells], halo_f.at[2 * ye : 2 * ye + ze],
            f_send.at[2], f_recv.at[2], up_z,
        ),
        send(
            flux.at[2, 0:ze], halo_f.at[2 * ye + ze : 2 * ye + 2 * ze],
            f_send.at[3], f_recv.at[3], down_z,
        ),
    ]
    f0 = split(flux[0])
    div[...] = (
        dot(f0[0], along_x[...]) + dot(f0[1], along_x[...])
        + dot(own[0:cells], f1[0]) + dot(own[0:cells], f1[1])
        + dot(own[cells:], f2[0]) + dot(own[cells:], f2[1])
    )
    load_big.wait()
    load_plane.wait()
    for copy in halo_copies:
        copy.wait()
    h = split(halo_f[...])
    d = split((div[...] + dot(beside_sum[...], h[0]) + dot(beside_sum[...], h[1])) * sixtieth)

    def spread(buffer):
        if rows2 % 8 == 0:
            buffer[...] = line[...].reshape(owners, rows2, cells)
        else:
            for k in range(owners):
                buffer[k] = line[k * rows2 : (k + 1) * rows2, :]

    def gather(buffer):
        if rows2 % 8 == 0:
            return buffer[...].reshape(owners * rows2, cells)
        for k in range(owners):
            line[k * rows2 : (k + 1) * rows2, :] = buffer[k]
        return line[...]

    def exchange(source, target, send_sem, recv_sem, meanwhile):
        def copy_of(i):
            other = lax.rem(me + i, owners)
            return pltpu.make_async_remote_copy(
                src_ref=source.at[other], dst_ref=target.at[me],
                send_sem=send_sem.at[i], recv_sem=recv_sem.at[i],
                device_id=(other // gz, lax.rem(other, gz)), device_id_type=mesh_ids,
            )

        def begin(i, carry):
            copy_of(i).start()
            return carry

        def end(i, carry):
            copy_of(i).wait()
            return carry

        lax.fori_loop(1, owners, begin, 0)
        target[me] = source[me]
        meanwhile()
        lax.fori_loop(1, owners, end, 0)

    def make_factor():
        row = lax.broadcasted_iota(jnp.int32, (2 * m * owners // 2, cells), 0)
        mode = me * m + (row & (m - 1))
        u = (mode - lx // 4).astype(jnp.float32) * (2.0 * np.pi / lx)
        v = u * u
        sine = jnp.zeros_like(u)
        cosine = jnp.zeros_like(u)
        for n in range(9, -1, -1):
            sign = -1.0 if n % 2 else 1.0
            sine = sine * v + sign / float(np.prod(np.arange(1.0, 2 * n + 1)))
            cosine = cosine * v + sign / float(np.prod(np.arange(1.0, 2 * n + 2)))
        cosine = -u * cosine
        kx = (
            1.5 * sine - 0.6 * sine * cosine + sine * (3.0 - 4.0 * sine * sine) * (1.0 / 30.0)
        )
        zero_mode = mode == 0
        kx = jnp.where(zero_mode, 0.0, kx)
        ky, kz = plane[2], plane[3]
        symbol = jnp.zeros_like(kx)
        for c in range(3):
            mixed = metric[c, 0] * kx + metric[c, 1] * ky + metric[c, 2] * kz
            symbol = symbol + mixed * mixed
        at_edge = zero_mode & (plane[4] > 0.5)
        total = float(lx * ey * gy * ez * gz)
        factor[...] = jnp.where(at_edge, 0.0, -1.0 / (jnp.where(at_edge, 1.0, symbol) * total))

    line[...] = dot3((big[0], big[1]), d, 1, 1)
    spread(there)
    exchange(there, here, a_send, a_recv, make_factor)

    half = lx // 2
    out = dot3((big[4], big[5]), split(gather(here)))
    re, im = out[:half], out[half:]
    tr, ti = plane[0], plane[1]
    both = jnp.concatenate([re * tr - im * ti, re * ti + im * tr], axis=1)
    out = dot3(split(both), (big[8], big[9]))
    re, im = out[:, :cells] * factor[...], out[:, cells:] * factor[...]
    both = jnp.concatenate([re, im], axis=1)
    out = dot3(split(both), (big[10], big[11]))
    re, im = out[:, :cells], out[:, cells:]
    both = jnp.concatenate([re * tr + im * ti, im * tr - re * ti], axis=0)
    line[...] = dot3((big[6], big[7]), split(both))
    spread(there2)
    exchange(there2, here2, b_send, b_recv, lambda: None)

    press[...] = dot3(split(gather(here2)), (big[2], big[3]), 0, 0)
    p = split(press[...], 3)
    edge_p[...] = dot(pick[...], p[0]) + dot(pick[...], p[1]) + dot(pick[...], p[2])
    halo_copies = [
        send(edge_p.at[0:ye], halo_p.at[0:ye], p_send.at[0], p_recv.at[0], up_y),
        send(edge_p.at[ye : 2 * ye], halo_p.at[ye : 2 * ye], p_send.at[1], p_recv.at[1], down_y),
        send(
            press.at[cells - ze : cells], halo_p.at[2 * ye : 2 * ye + ze],
            p_send.at[2], p_recv.at[2], up_z,
        ),
        send(
            press.at[0:ze], halo_p.at[2 * ye + ze : 2 * ye + 2 * ze],
            p_send.at[3], p_recv.at[3], down_z,
        ),
    ]
    grad[0] = dot(own[...], p[0]) + dot(own[...], p[1]) + dot(own[...], p[2])
    grad_x[0] = dot(p[0], along_x[...]) + dot(p[1], along_x[...]) + dot(p[2], along_x[...])
    for copy in halo_copies:
        copy.wait()
    h = split(halo_p[...], 3)
    grad[0] += dot(beside[...], h[0]) + dot(beside[...], h[1]) + dot(beside[...], h[2])

    def project(i, carry):
        rows = pl.ds(pl.multiple_of(i * 16, 16), 16)
        rows_z = pl.ds(pl.multiple_of(cells + i * 16, 16), 16)
        push = [
            grad_x[0, rows, :] * sixtieth, grad[0, rows, :] * sixtieth, grad[0, rows_z, :] * sixtieth
        ]
        for c in range(3):
            motion[c, rows, :] = prov[c, rows, :] - (
                metric[c, 0] * push[0] + metric[c, 1] * push[1] + metric[c, 2] * push[2]
            )
        return carry

    lax.fori_loop(0, cells // 16, project, 0)


def shards(flow_state, metric, deformation):
    gy, gz = lax.axis_size("gy"), lax.axis_size("gz")
    owners = gy * gz
    _, ez, ey, lx = flow_state.shape
    cells = ez * ey
    m = lx // 2 // owners
    own, beside, pick, along_x = stencil_tables(ez, ey, lx)
    cos_x, sin_x, weight = x_tables(lx)
    ahead = by_owner(cos_x, sin_x, owners)
    back = by_owner(cos_x * weight, sin_x * weight, owners)
    twist, kron, block, ky, kz, edge = plane_tables(gy, gz, ey, ez)
    eye = np.eye(m)
    br, bi = np.cos(block), np.sin(block)
    pair = np.stack([np.stack([br, -bi], 1), np.stack([bi, br], 1)], 0)
    across = np.einsum("atsb,mn->atmsbn", pair.transpose(0, 1, 3, 2), eye)
    across = across.reshape(lx, lx)
    wr, wi = np.cos(kron), np.sin(kron)
    within = np.block([[wr, wi], [-wi, wr]])
    big = np.stack(
        halves(ahead) + halves(back) + halves(across) + halves(across.T)
        + halves(within) + halves(within.T)
    )
    plane = np.repeat(
        np.stack([np.cos(twist), np.sin(twist), ky, kz, edge.astype(np.float64)]), m, axis=1
    ).astype(np.float32)
    bf = jnp.bfloat16
    f32 = jnp.float32
    vmem = pl.BlockSpec(memory_space=pltpu.VMEM)
    smem = pl.BlockSpec(memory_space=pltpu.SMEM)
    hbm = pl.BlockSpec(memory_space=pl.ANY)
    wide = 6 * ez + 8 * ey
    dma = pltpu.SemaphoreType.DMA
    motion, heat_next = pl.pallas_call(
        lambda *refs: kernel((gy, gz, ez, ey, lx), *refs),
        out_shape=(
            jax.ShapeDtypeStruct((3, cells, lx), f32), jax.ShapeDtypeStruct((cells, lx), f32)
        ),
        in_specs=[smem, smem] + [vmem] * 6 + [hbm] * 2,
        out_specs=(vmem, vmem),
        scratch_shapes=[
            pltpu.VMEM(big.shape, bf),
            pltpu.VMEM(plane.shape, f32),
            pltpu.VMEM((2, 4, 3 * ez, lx), bf),
            pltpu.VMEM((4, wide, lx), bf),
            pltpu.VMEM((4, 2 * cells, lx), f32),
            pltpu.VMEM((4, cells, lx), f32),
            pltpu.VMEM((3, cells, lx), f32),
            pltpu.VMEM((3, cells, lx), f32),
            pltpu.VMEM((6 * ez, lx), f32),
            pltpu.VMEM((wide, lx), f32),
            pltpu.VMEM((cells, lx), f32),
            pltpu.VMEM((6 * ez, lx), f32),
            pltpu.VMEM((wide, lx), f32),
            pltpu.VMEM((cells, lx), f32),
            pltpu.VMEM((lx, cells), f32),
        ]
        + [pltpu.VMEM((owners, 2 * m, cells), f32)] * 4
        + [pltpu.VMEM((lx // 2, cells), f32)]
        + [dma((2,))] + [dma((4,))] * 6 + [dma((owners,))] * 4,
        compiler_params=pltpu.CompilerParams(
            collective_id=0, has_side_effects=True, vmem_limit_bytes=56 * 2**20
        ),
        cost_estimate=pl.CostEstimate(
            flops=4 * 10**9, bytes_accessed=12 * 2**20, transcendentals=0
        ),
        name="substep",
    )(
        metric, deformation, flow_state.reshape(4, cells, lx),
        jnp.asarray(own, bf), jnp.asarray(beside, bf),
        jnp.asarray(beside[:cells] + beside[cells:], bf), jnp.asarray(pick, bf),
        jnp.asarray(along_x, bf), jnp.asarray(big), jnp.asarray(plane),
    )
    return motion.reshape(3, ez, ey, lx), heat_next.reshape(ez, ey, lx)

def solution(mesh):
    placed = (P(None, "gz", "gy", None), P(), P())
    return jax.shard_map(
        shards,
        mesh=mesh,
        in_specs=placed,
        out_specs=(P(None, "gz", "gy", None), P("gz", "gy", None)),
        check_vma=False,
    )
```

```python
import numpy as np

import jax
import jax.numpy as jnp
from jax import lax
from jax.experimental import pallas as pl
from jax.experimental.pallas import tpu as pltpu
from jax.sharding import PartitionSpec as P

substep_width = 0.4
parts = 2
mesh_ids = pl.DeviceIdType.MESH
coefs = {1: 45.0, 2: -9.0, 3: 1.0, -1: -45.0, -2: 9.0, -3: -1.0}


def x_tables(length):
    half = length // 2
    k = np.arange(half)[:, None]
    x = np.arange(length)[None, :]
    angle = 2.0 * np.pi * ((k * x) % length) / length
    c, s = np.cos(angle), -np.sin(angle)
    s[0] = np.where(np.arange(length) % 2 == 0, 1.0, -1.0)
    weight = np.where(np.arange(half) == 0, 1.0, 2.0)[:, None]
    return c, s, weight


def by_owner(re, im, owners):
    half, length = re.shape
    m = half // owners
    return np.concatenate(
        [re.reshape(owners, m, length), im.reshape(owners, m, length)], axis=1
    ).reshape(2 * half, length)


def wave(m, length):
    a = 2.0 * np.pi * m / length
    value = 1.5 * np.sin(a) - 0.3 * np.sin(2 * a) + np.sin(3 * a) / 30.0
    return np.where((2 * m) % length == 0, 0.0, value)


def plane_tables(gy, gz, ey, ez):
    ly, lz = gy * ey, gz * ez
    b = np.repeat(np.arange(ez), ey)
    e = np.tile(np.arange(ey), ez)
    s = np.repeat(np.arange(gy), gz)[:, None]
    q = np.tile(np.arange(gz), gy)[:, None]
    twist = -2.0 * np.pi * (b * q / lz + e * s / ly)
    kron = -2.0 * np.pi * (np.outer(b, b) / ez + np.outer(e, e) / ey)
    my = gy * e[None, :] + s
    mz = gz * b[None, :] + q
    block = -2.0 * np.pi * (
        np.outer(s, s) / gy + np.outer(q, q) / gz
    )
    edge = ((2 * my) % ly == 0) & ((2 * mz) % lz == 0)
    return twist, kron, block, wave(my, ly), wave(mz, lz), edge


def stencil_tables(ez, ey, lx):
    cells, zc = ez * ey, ez // parts
    part = zc * ey
    own = np.zeros((2 * cells, cells))
    beside = np.zeros((parts, 2 * part, 6 * zc + 4 * ey))
    pick = np.zeros((6 * zc, part))
    for z in range(ez):
        h, zh = z // zc, z % zc
        for y in range(ey):
            r, rh = z * ey + y, zh * ey + y
            for o, w in coefs.items():
                t = y + o
                if 0 <= t < ey:
                    own[r, z * ey + t] += w
                elif t < 0:
                    beside[h, rh, (t + 3) * zc + zh] += w
                else:
                    beside[h, rh, (3 + t - ey) * zc + zh] += w
                t = z + o
                if 0 <= t < ez:
                    own[cells + r, t * ey + y] += w
                elif t < 0:
                    beside[h, part + rh, 6 * zc + (t + 4) * ey + y] += w
                else:
                    beside[h, part + rh, 6 * zc + (t - ez) * ey + y] += w
        for j in range(3):
            pick[j * zc + zh, zh * ey + ey - 3 + j] = 1.0
            pick[(3 + j) * zc + zh, zh * ey + j] = 1.0
    along_x = np.zeros((lx, lx))
    for o, w in coefs.items():
        x = np.arange(lx)
        along_x[(x + o) % lx, x] += w
    return own, beside, pick, along_x


def halves(a):
    a = np.asarray(a, np.float32)
    top = a.astype(jnp.bfloat16)
    return [top, (a - top.astype(np.float32)).astype(jnp.bfloat16)]


def split(x, pieces=2):
    out = []
    for _ in range(pieces):
        top = x.astype(jnp.bfloat16)
        out.append(top)
        x = x - top.astype(jnp.float32)
    return out


def dot(a, b, ca=1, cb=0):
    return lax.dot_general(a, b, (((ca,), (cb,)), ((), ())), preferred_element_type=jnp.float32)


def dot3(a, b, ca=1, cb=0):
    return dot(a[0], b[0], ca, cb) + dot(a[0], b[1], ca, cb) + dot(a[1], b[0], ca, cb)


def kernel(
    sizes, metric, deform, state, own, beside, beside_sum, pick, along_x, big_hbm, plane_hbm,
    motion, heat_next,
    big, plane, edge_state, halo_state, grad, grad_x, prov, flux, edge_f, halo_f, div,
    edge_p, halo_p, press, line, there, here, there2, here2, factor,
    load_sem, s_send, s_recv, f_send, f_recv, p_send, p_recv, a_send, a_recv, b_send, b_recv,
):
    gy, gz, ez, ey, lx = sizes
    owners = gy * gz
    cells = ez * ey
    rows2 = lx // owners
    m = rows2 // 2
    zc = ez // parts
    part = zc * ey
    ye, ze = 3 * zc, 4 * ey
    last = parts - 1
    iy, iz = lax.axis_index("gy"), lax.axis_index("gz")
    me = iy * gz + iz
    up_y = (lax.rem(iy + 1, gy), iz)
    down_y = (lax.rem(iy + gy - 1, gy), iz)
    up_z = (iy, lax.rem(iz + 1, gz))
    down_z = (iy, lax.rem(iz + gz - 1, gz))

    load_big = pltpu.make_async_copy(big_hbm, big, load_sem.at[0])
    load_plane = pltpu.make_async_copy(plane_hbm, plane, load_sem.at[1])
    load_big.start()
    load_plane.start()

    barrier = pltpu.get_barrier_semaphore()

    def greet(i, carry):
        other = lax.rem(me + i, owners)
        pl.semaphore_signal(
            barrier, inc=1, device_id=(other // gz, lax.rem(other, gz)), device_id_type=mesh_ids
        )
        return carry

    lax.fori_loop(1, owners, greet, 0)

    for h in range(parts):
        for c in range(4):
            picked = dot(pick[...], state[c, h * part : (h + 1) * part]).astype(jnp.bfloat16)
            edge_state[h, 0, c] = picked[:ye]
            edge_state[h, 1, c] = picked[ye:]
    pl.semaphore_wait(barrier, owners - 1)

    def send(src, dst, send_sem, recv_sem, to):
        copy = pltpu.make_async_remote_copy(
            src_ref=src, dst_ref=dst, send_sem=send_sem, recv_sem=recv_sem,
            device_id=to, device_id_type=mesh_ids,
        )
        copy.start()
        return copy

    side_z = [
        send(
            state.at[:, cells - ze : cells], halo_state.at[0, :, 2 * ye : 2 * ye + ze],
            s_send.at[2 * parts], s_recv.at[2 * parts], up_z,
        ),
        send(
            state.at[:, 0:ze], halo_state.at[last, :, 2 * ye : 2 * ye + ze],
            s_send.at[2 * parts + 1], s_recv.at[2 * parts + 1], down_z,
        ),
    ]
    side_y = [
        [
            send(
                edge_state.at[h, w], halo_state.at[h, :, w * ye : (w + 1) * ye],
                s_send.at[2 * h + w], s_recv.at[2 * h + w], (up_y, down_y)[w],
            )
            for w in range(2)
        ]
        for h in range(parts)
    ]
    for c in range(4):
        grad[c] = dot(own[...], state[c])
        grad_x[c] = dot(state[c], along_x[...])

    def borders(field, edges, halo, sends, recvs):
        def side(h):
            return [
                send(
                    edges.at[h, w * ye : (w + 1) * ye], halo.at[h, w * ye : (w + 1) * ye],
                    sends.at[2 * h + w], recvs.at[2 * h + w], (up_y, down_y)[w],
                )
                for w in range(2)
            ]

        def low():
            return send(
                field.at[0:ze], halo.at[last, 2 * ye : 2 * ye + ze],
                sends.at[2 * parts + 1], recvs.at[2 * parts + 1], down_z,
            )

        def top():
            return send(
                field.at[cells - ze : cells], halo.at[0, 2 * ye : 2 * ye + ze],
                sends.at[2 * parts], recvs.at[2 * parts], up_z,
            )

        return side, low, top

    sixtieth = 1.0 / 60.0

    def advance(i, carry):
        rows = pl.ds(pl.multiple_of(i * 16, 16), 16)
        rows_z = pl.ds(pl.multiple_of(cells + i * 16, 16), 16)
        f = [state[c, rows, :].astype(jnp.float32) for c in range(4)]
        contra = [
            (metric[0, j] * f[0] + metric[1, j] * f[1] + metric[2, j] * f[2]) * sixtieth
            for j in range(3)
        ]
        carried = [
            contra[0] * grad_x[c, rows, :]
            + contra[1] * grad[c, rows, :]
            + contra[2] * grad[c, rows_z, :]
            for c in range(4)
        ]
        new = []
        for c in range(3):
            change = -carried[c] - (
                deform[c, 0] * f[0] + deform[c, 1] * f[1] + deform[c, 2] * f[2]
            )
            if c == 2:
                change = change + f[3]
            new.append(f[c] + substep_width * change)
            prov[c, rows, :] = new[c]
        heat_next[rows, :] = f[3] + substep_width * (-carried[3] - f[2])
        for j in range(3):
            flux[j, rows, :] = metric[0, j] * new[0] + metric[1, j] * new[1] + metric[2, j] * new[2]
        return carry

    side_f, low_f, top_f = borders(flux.at[2], edge_f, halo_f, f_send, f_recv)
    f_side = []
    for h in range(parts):
        for copy in side_y[h]:
            copy.wait()
        if h == 0:
            for copy in side_z:
                copy.wait()
        lo, hi = h * part, (h + 1) * part
        for c in range(4):
            more = dot(beside[h], halo_state[h, c])
            grad[c, lo:hi] += more[:part]
            grad[c, cells + lo : cells + hi] += more[part:]
        lax.fori_loop(lo // 16, hi // 16, advance, 0)
        f1 = split(flux[1, lo:hi])
        edge_f[h] = dot(pick[...], f1[0]) + dot(pick[...], f1[1])
        f_side.append(side_f(h))
        if h == 0:
            f_low = low_f()
    f_top = top_f()

    f0 = split(flux[0])
    f1 = split(flux[1])
    f2 = split(flux[2])
    div[...] = (
        dot(f0[0], along_x[...]) + dot(f0[1], along_x[...])
        + dot(own[0:cells], f1[0]) + dot(own[0:cells], f1[1])
        + dot(own[cells:], f2[0]) + dot(own[cells:], f2[1])
    )
    load_big.wait()
    load_plane.wait()

    def spread(buffer, lo, hi):
        if rows2 % 8 == 0:
            buffer[:, :, lo:hi] = line[:, lo:hi].reshape(owners, rows2, hi - lo)
        else:
            for k in range(owners):
                buffer[k, :, lo:hi] = line[k * rows2 : (k + 1) * rows2, lo:hi]

    def gather(buffer, lo, hi):
        if rows2 % 8 == 0:
            return buffer[:, :, lo:hi].reshape(owners * rows2, hi - lo)
        for k in range(owners):
            line[k * rows2 : (k + 1) * rows2, lo:hi] = buffer[k, :, lo:hi]
        return line[:, lo:hi]

    def exchange(source, target, send_sem, recv_sem, h):
        lanes = slice(h * part, (h + 1) * part)

        def copy_of(i):
            other = lax.rem(me + i, owners)
            return pltpu.make_async_remote_copy(
                src_ref=source.at[other, :, lanes], dst_ref=target.at[me, :, lanes],
                send_sem=send_sem.at[h, i], recv_sem=recv_sem.at[h, i],
                device_id=(other // gz, lax.rem(other, gz)), device_id_type=mesh_ids,
            )

        def begin(i, carry):
            copy_of(i).start()
            return carry

        def end(i, carry):
            copy_of(i).wait()
            return carry

        lax.fori_loop(1, owners, begin, 0)
        target[me, :, lanes] = source[me, :, lanes]
        return lambda: lax.fori_loop(1, owners, end, 0)

    def make_factor():
        row = lax.broadcasted_iota(jnp.int32, (2 * m * owners // 2, cells), 0)
        mode = me * m + (row & (m - 1))
        u = (mode - lx // 4).astype(jnp.float32) * (2.0 * np.pi / lx)
        v = u * u
        sine = jnp.zeros_like(u)
        cosine = jnp.zeros_like(u)
        for n in range(9, -1, -1):
            sign = -1.0 if n % 2 else 1.0
            sine = sine * v + sign / float(np.prod(np.arange(1.0, 2 * n + 1)))
            cosine = cosine * v + sign / float(np.prod(np.arange(1.0, 2 * n + 2)))
        cosine = -u * cosine
        kx = (
            1.5 * sine - 0.6 * sine * cosine + sine * (3.0 - 4.0 * sine * sine) * (1.0 / 30.0)
        )
        zero_mode = mode == 0
        kx = jnp.where(zero_mode, 0.0, kx)
        ky, kz = plane[2], plane[3]
        symbol = jnp.zeros_like(kx)
        for c in range(3):
            mixed = metric[c, 0] * kx + metric[c, 1] * ky + metric[c, 2] * kz
            symbol = symbol + mixed * mixed
        at_edge = zero_mode & (plane[4] > 0.5)
        total = float(lx * ey * gy * ez * gz)
        factor[...] = jnp.where(at_edge, 0.0, -1.0 / (jnp.where(at_edge, 1.0, symbol) * total))

    pending = []
    for h in range(parts):
        for copy in f_side[h]:
            copy.wait()
        if h == 0:
            f_top.wait()
        if h == last:
            f_low.wait()
        lo, hi = h * part, (h + 1) * part
        e = split(halo_f[h])
        d = split((div[lo:hi] + dot(beside_sum[h], e[0]) + dot(beside_sum[h], e[1])) * sixtieth)
        line[:, lo:hi] = dot3((big[0], big[1]), d, 1, 1)
        spread(there, lo, hi)
        pending.append(exchange(there, here, a_send, a_recv, h))
    make_factor()
    for done in pending:
        done()

    half = lx // 2
    out = dot3((big[4], big[5]), split(gather(here, 0, cells)))
    re, im = out[:half], out[half:]
    tr, ti = plane[0], plane[1]
    both = jnp.concatenate([re * tr - im * ti, re * ti + im * tr], axis=1)
    out = dot3(split(both), (big[8], big[9]))
    re, im = out[:, :cells] * factor[...], out[:, cells:] * factor[...]
    both = jnp.concatenate([re, im], axis=1)
    out = dot3(split(both), (big[10], big[11]))
    re, im = out[:, :cells], out[:, cells:]
    both = jnp.concatenate([re * tr + im * ti, im * tr - re * ti], axis=0)
    line[...] = dot3((big[6], big[7]), split(both))
    pending = []
    for h in range(parts):
        spread(there2, h * part, (h + 1) * part)
        pending.append(exchange(there2, here2, b_send, b_recv, h))
    side_p, low_p, top_p = borders(press, edge_p, halo_p, p_send, p_recv)
    p_side = []
    for h in range(parts):
        pending[h]()
        lo, hi = h * part, (h + 1) * part
        press[lo:hi] = dot3(split(gather(here2, lo, hi)), (big[2], big[3]), 0, 0)
        p = split(press[lo:hi], 3)
        edge_p[h] = dot(pick[...], p[0]) + dot(pick[...], p[1]) + dot(pick[...], p[2])
        p_side.append(side_p(h))
        if h == 0:
            p_low = low_p()
    p_top = top_p()
    p = split(press[...], 3)
    grad[0] = dot(own[...], p[0]) + dot(own[...], p[1]) + dot(own[...], p[2])
    grad_x[0] = dot(p[0], along_x[...]) + dot(p[1], along_x[...]) + dot(p[2], along_x[...])
    for h in range(parts):
        for copy in p_side[h]:
            copy.wait()
        if h == 0:
            p_top.wait()
        if h == last:
            p_low.wait()
        lo, hi = h * part, (h + 1) * part
        e = split(halo_p[h], 3)
        more = dot(beside[h], e[0]) + dot(beside[h], e[1]) + dot(beside[h], e[2])
        grad[0, lo:hi] += more[:part]
        grad[0, cells + lo : cells + hi] += more[part:]

    def project(i, carry):
        rows = pl.ds(pl.multiple_of(i * 16, 16), 16)
        rows_z = pl.ds(pl.multiple_of(cells + i * 16, 16), 16)
        push = [
            grad_x[0, rows, :] * sixtieth, grad[0, rows, :] * sixtieth, grad[0, rows_z, :] * sixtieth
        ]
        for c in range(3):
            motion[c, rows, :] = prov[c, rows, :] - (
                metric[c, 0] * push[0] + metric[c, 1] * push[1] + metric[c, 2] * push[2]
            )
        return carry

    lax.fori_loop(0, cells // 16, project, 0)


def shards(flow_state, metric, deformation):
    gy, gz = lax.axis_size("gy"), lax.axis_size("gz")
    owners = gy * gz
    _, ez, ey, lx = flow_state.shape
    cells = ez * ey
    m = lx // 2 // owners
    own, beside, pick, along_x = stencil_tables(ez, ey, lx)
    cos_x, sin_x, weight = x_tables(lx)
    ahead = by_owner(cos_x, sin_x, owners)
    back = by_owner(cos_x * weight, sin_x * weight, owners)
    twist, kron, block, ky, kz, edge = plane_tables(gy, gz, ey, ez)
    eye = np.eye(m)
    br, bi = np.cos(block), np.sin(block)
    pair = np.stack([np.stack([br, -bi], 1), np.stack([bi, br], 1)], 0)
    across = np.einsum("atsb,mn->atmsbn", pair.transpose(0, 1, 3, 2), eye)
    across = across.reshape(lx, lx)
    wr, wi = np.cos(kron), np.sin(kron)
    within = np.block([[wr, wi], [-wi, wr]])
    big = np.stack(
        halves(ahead) + halves(back) + halves(across) + halves(across.T)
        + halves(within) + halves(within.T)
    )
    plane = np.repeat(
        np.stack([np.cos(twist), np.sin(twist), ky, kz, edge.astype(np.float64)]), m, axis=1
    ).astype(np.float32)
    bf = jnp.bfloat16
    f32 = jnp.float32
    vmem = pl.BlockSpec(memory_space=pltpu.VMEM)
    smem = pl.BlockSpec(memory_space=pltpu.SMEM)
    hbm = pl.BlockSpec(memory_space=pl.ANY)
    zc = ez // parts
    wide = 6 * zc + 4 * ey
    part = zc * ey
    dma = pltpu.SemaphoreType.DMA
    motion, heat_next = pl.pallas_call(
        lambda *refs: kernel((gy, gz, ez, ey, lx), *refs),
        out_shape=(
            jax.ShapeDtypeStruct((3, cells, lx), f32), jax.ShapeDtypeStruct((cells, lx), f32)
        ),
        in_specs=[smem, smem] + [vmem] * 6 + [hbm] * 2,
        out_specs=(vmem, vmem),
        scratch_shapes=[
            pltpu.VMEM(big.shape, bf),
            pltpu.VMEM(plane.shape, f32),
            pltpu.VMEM((parts, 2, 4, 3 * zc, lx), bf),
            pltpu.VMEM((parts, 4, wide, lx), bf),
            pltpu.VMEM((4, 2 * cells, lx), f32),
            pltpu.VMEM((4, cells, lx), f32),
            pltpu.VMEM((3, cells, lx), f32),
            pltpu.VMEM((3, cells, lx), f32),
            pltpu.VMEM((parts, 6 * zc, lx), f32),
            pltpu.VMEM((parts, wide, lx), f32),
            pltpu.VMEM((cells, lx), f32),
            pltpu.VMEM((parts, 6 * zc, lx), f32),
            pltpu.VMEM((parts, wide, lx), f32),
            pltpu.VMEM((cells, lx), f32),
            pltpu.VMEM((lx, cells), f32),
        ]
        + [pltpu.VMEM((owners, 2 * m, cells), f32)] * 4
        + [pltpu.VMEM((lx // 2, cells), f32)]
        + [dma((2,))] + [dma((2 * parts + 2,))] * 6 + [dma((parts, owners))] * 4,
        compiler_params=pltpu.CompilerParams(
            collective_id=0, has_side_effects=True, vmem_limit_bytes=56 * 2**20
        ),
        cost_estimate=pl.CostEstimate(
            flops=4 * 10**9, bytes_accessed=12 * 2**20, transcendentals=0
        ),
        name="substep",
    )(
        metric, deformation, flow_state.reshape(4, cells, lx),
        jnp.asarray(own, bf), jnp.asarray(beside, bf),
        jnp.asarray(beside[:, :part] + beside[:, part:], bf), jnp.asarray(pick, bf),
        jnp.asarray(along_x, bf), jnp.asarray(big), jnp.asarray(plane),
    )
    return motion.reshape(3, ez, ey, lx), heat_next.reshape(ez, ey, lx)

def solution(mesh):
    placed = (P(None, "gz", "gy", None), P(), P())
    return jax.shard_map(
        shards,
        mesh=mesh,
        in_specs=placed,
        out_specs=(P(None, "gz", "gy", None), P("gz", "gy", None)),
        check_vma=False,
    )
```

```python
import numpy as np

import jax
import jax.numpy as jnp
from jax import lax
from jax.experimental import pallas as pl
from jax.experimental.pallas import tpu as pltpu
from jax.sharding import PartitionSpec as P

substep_width = 0.4
parts = 2
mesh_ids = pl.DeviceIdType.MESH
coefs = {1: 45.0, 2: -9.0, 3: 1.0, -1: -45.0, -2: 9.0, -3: -1.0}


def x_tables(length):
    half = length // 2
    k = np.arange(half)[:, None]
    x = np.arange(length)[None, :]
    angle = 2.0 * np.pi * ((k * x) % length) / length
    c, s = np.cos(angle), -np.sin(angle)
    s[0] = np.where(np.arange(length) % 2 == 0, 1.0, -1.0)
    weight = np.where(np.arange(half) == 0, 1.0, 2.0)[:, None]
    return c, s, weight


def by_owner(re, im, owners):
    half, length = re.shape
    m = half // owners
    return np.concatenate(
        [re.reshape(owners, m, length), im.reshape(owners, m, length)], axis=1
    ).reshape(2 * half, length)


def wave(m, length):
    a = 2.0 * np.pi * m / length
    value = 1.5 * np.sin(a) - 0.3 * np.sin(2 * a) + np.sin(3 * a) / 30.0
    return np.where((2 * m) % length == 0, 0.0, value)


def plane_tables(gy, gz, ey, ez):
    ly, lz = gy * ey, gz * ez
    b = np.repeat(np.arange(ez), ey)
    e = np.tile(np.arange(ey), ez)
    s = np.repeat(np.arange(gy), gz)[:, None]
    q = np.tile(np.arange(gz), gy)[:, None]
    twist = -2.0 * np.pi * (b * q / lz + e * s / ly)
    kron = -2.0 * np.pi * (np.outer(b, b) / ez + np.outer(e, e) / ey)
    my = gy * e[None, :] + s
    mz = gz * b[None, :] + q
    block = -2.0 * np.pi * (
        np.outer(s, s) / gy + np.outer(q, q) / gz
    )
    edge = ((2 * my) % ly == 0) & ((2 * mz) % lz == 0)
    return twist, kron, block, wave(my, ly), wave(mz, lz), edge


def stencil_tables(ez, ey, lx):
    cells, zc = ez * ey, ez // parts
    part = zc * ey
    own = np.zeros((2 * cells, cells))
    beside = np.zeros((parts, 2 * part, 6 * zc + 4 * ey))
    pick = np.zeros((6 * zc, part))
    for z in range(ez):
        h, zh = z // zc, z % zc
        for y in range(ey):
            r, rh = z * ey + y, zh * ey + y
            for o, w in coefs.items():
                t = y + o
                if 0 <= t < ey:
                    own[r, z * ey + t] += w
                elif t < 0:
                    beside[h, rh, (t + 3) * zc + zh] += w
                else:
                    beside[h, rh, (3 + t - ey) * zc + zh] += w
                t = z + o
                if 0 <= t < ez:
                    own[cells + r, t * ey + y] += w
                elif t < 0:
                    beside[h, part + rh, 6 * zc + (t + 4) * ey + y] += w
                else:
                    beside[h, part + rh, 6 * zc + (t - ez) * ey + y] += w
        for j in range(3):
            pick[j * zc + zh, zh * ey + ey - 3 + j] = 1.0
            pick[(3 + j) * zc + zh, zh * ey + j] = 1.0
    along_x = np.zeros((lx, lx))
    for o, w in coefs.items():
        x = np.arange(lx)
        along_x[(x + o) % lx, x] += w
    return own, beside, pick, along_x


def halves(a):
    a = np.asarray(a, np.float32)
    top = a.astype(jnp.bfloat16)
    return [top, (a - top.astype(np.float32)).astype(jnp.bfloat16)]


def split(x, pieces=2):
    out = []
    for _ in range(pieces):
        top = x.astype(jnp.bfloat16)
        out.append(top)
        x = x - top.astype(jnp.float32)
    return out


def dot(a, b, ca=1, cb=0):
    return lax.dot_general(a, b, (((ca,), (cb,)), ((), ())), preferred_element_type=jnp.float32)


def dot3(a, b, ca=1, cb=0):
    return dot(a[0], b[0], ca, cb) + dot(a[0], b[1], ca, cb) + dot(a[1], b[0], ca, cb)


def kernel(
    sizes, metric, deform, state, own, beside, beside_sum, pick, along_x, big_hbm, plane_hbm,
    motion, heat_next,
    big, plane, edge_state, halo_state, grad, grad_x, prov, flux, edge_f, halo_f, div,
    edge_p, halo_p, press, line, there, here, there2, here2, factor,
    load_sem, s_send, s_recv, f_send, f_recv, p_send, p_recv, a_send, a_recv, b_send, b_recv,
):
    gy, gz, ez, ey, lx = sizes
    owners = gy * gz
    cells = ez * ey
    rows2 = lx // owners
    m = rows2 // 2
    zc = ez // parts
    part = zc * ey
    ye, ze = 3 * zc, 4 * ey
    last = parts - 1
    iy, iz = lax.axis_index("gy"), lax.axis_index("gz")
    me = iy * gz + iz
    up_y = (lax.rem(iy + 1, gy), iz)
    down_y = (lax.rem(iy + gy - 1, gy), iz)
    up_z = (iy, lax.rem(iz + 1, gz))
    down_z = (iy, lax.rem(iz + gz - 1, gz))

    load_big = pltpu.make_async_copy(big_hbm, big, load_sem.at[0])
    load_plane = pltpu.make_async_copy(plane_hbm, plane, load_sem.at[1])
    load_big.start()
    load_plane.start()

    def to_all(begin):
        for dz in range(1, gz):
            begin(iy, lax.rem(iz + dz, gz))

        def ring(dy, carry):
            oy = lax.rem(iy + dy, gy)
            for dz in range(gz):
                begin(oy, lax.rem(iz + dz, gz))
            return carry

        lax.fori_loop(1, gy, ring, 0)

    barrier = pltpu.get_barrier_semaphore()

    def greet(oy, oz):
        pl.semaphore_signal(barrier, inc=1, device_id=(oy, oz), device_id_type=mesh_ids)

    to_all(greet)

    for h in range(parts):
        for c in range(4):
            picked = dot(pick[...], state[c, h * part : (h + 1) * part]).astype(jnp.bfloat16)
            edge_state[h, 0, c] = picked[:ye]
            edge_state[h, 1, c] = picked[ye:]
    pl.semaphore_wait(barrier, owners - 1)

    def send(src, dst, send_sem, recv_sem, to):
        copy = pltpu.make_async_remote_copy(
            src_ref=src, dst_ref=dst, send_sem=send_sem, recv_sem=recv_sem,
            device_id=to, device_id_type=mesh_ids,
        )
        copy.start()
        return copy

    side_z = [
        send(
            state.at[:, cells - ze : cells], halo_state.at[0, :, 2 * ye : 2 * ye + ze],
            s_send.at[2 * parts], s_recv.at[2 * parts], up_z,
        ),
        send(
            state.at[:, 0:ze], halo_state.at[last, :, 2 * ye : 2 * ye + ze],
            s_send.at[2 * parts + 1], s_recv.at[2 * parts + 1], down_z,
        ),
    ]
    side_y = [
        [
            send(
                edge_state.at[h, w], halo_state.at[h, :, w * ye : (w + 1) * ye],
                s_send.at[2 * h + w], s_recv.at[2 * h + w], (up_y, down_y)[w],
            )
            for w in range(2)
        ]
        for h in range(parts)
    ]
    for c in range(4):
        grad[c] = dot(own[...], state[c])
        grad_x[c] = dot(state[c], along_x[...])

    def borders(field, edges, halo, sends, recvs):
        def side(h):
            return [
                send(
                    edges.at[h, w * ye : (w + 1) * ye], halo.at[h, w * ye : (w + 1) * ye],
                    sends.at[2 * h + w], recvs.at[2 * h + w], (up_y, down_y)[w],
                )
                for w in range(2)
            ]

        def low():
            return send(
                field.at[0:ze], halo.at[last, 2 * ye : 2 * ye + ze],
                sends.at[2 * parts + 1], recvs.at[2 * parts + 1], down_z,
            )

        def top():
            return send(
                field.at[cells - ze : cells], halo.at[0, 2 * ye : 2 * ye + ze],
                sends.at[2 * parts], recvs.at[2 * parts], up_z,
            )

        return side, low, top

    sixtieth = 1.0 / 60.0

    def advance(i, carry):
        rows = pl.ds(pl.multiple_of(i * 16, 16), 16)
        rows_z = pl.ds(pl.multiple_of(cells + i * 16, 16), 16)
        f = [state[c, rows, :].astype(jnp.float32) for c in range(4)]
        contra = [
            (metric[0, j] * f[0] + metric[1, j] * f[1] + metric[2, j] * f[2]) * sixtieth
            for j in range(3)
        ]
        carried = [
            contra[0] * grad_x[c, rows, :]
            + contra[1] * grad[c, rows, :]
            + contra[2] * grad[c, rows_z, :]
            for c in range(4)
        ]
        new = []
        for c in range(3):
            change = -carried[c] - (
                deform[c, 0] * f[0] + deform[c, 1] * f[1] + deform[c, 2] * f[2]
            )
            if c == 2:
                change = change + f[3]
            new.append(f[c] + substep_width * change)
            prov[c, rows, :] = new[c]
        heat_next[rows, :] = f[3] + substep_width * (-carried[3] - f[2])
        for j in range(3):
            flux[j, rows, :] = metric[0, j] * new[0] + metric[1, j] * new[1] + metric[2, j] * new[2]
        return carry

    side_f, low_f, top_f = borders(flux.at[2], edge_f, halo_f, f_send, f_recv)
    f_side = []
    for h in range(parts):
        for copy in side_y[h]:
            copy.wait()
        if h == 0:
            for copy in side_z:
                copy.wait()
        lo, hi = h * part, (h + 1) * part
        for c in range(4):
            more = dot(beside[h], halo_state[h, c])
            grad[c, lo:hi] += more[:part]
            grad[c, cells + lo : cells + hi] += more[part:]
        lax.fori_loop(lo // 16, hi // 16, advance, 0)
        f1 = split(flux[1, lo:hi])
        edge_f[h] = dot(pick[...], f1[0]) + dot(pick[...], f1[1])
        f_side.append(side_f(h))
        if h == 0:
            f_low = low_f()
    f_top = top_f()

    f0 = split(flux[0])
    f1 = split(flux[1])
    f2 = split(flux[2])
    div[...] = (
        dot(f0[0], along_x[...]) + dot(f0[1], along_x[...])
        + dot(own[0:cells], f1[0]) + dot(own[0:cells], f1[1])
        + dot(own[cells:], f2[0]) + dot(own[cells:], f2[1])
    )
    load_big.wait()
    load_plane.wait()

    def spread(buffer, h):
        lanes = slice(h * part, (h + 1) * part)
        if rows2 % 8 == 0:
            buffer[h] = line[:, lanes].reshape(owners, rows2, part)
        else:
            for k in range(owners):
                buffer[h, k] = line[k * rows2 : (k + 1) * rows2, lanes]

    def gather(buffer, h):
        if rows2 % 8 == 0:
            return buffer[h].reshape(owners * rows2, part)
        lanes = slice(h * part, (h + 1) * part)
        for k in range(owners):
            line[k * rows2 : (k + 1) * rows2, lanes] = buffer[h, k]
        return line[:, lanes]

    def exchange(source, target, send_sem, recv_sem, h):
        def begin(oy, oz):
            pltpu.make_async_remote_copy(
                src_ref=source.at[h, oy * gz + oz], dst_ref=target.at[h, me],
                send_sem=send_sem.at[h], recv_sem=recv_sem.at[h],
                device_id=(oy, oz), device_id_type=mesh_ids,
            ).start()

        to_all(begin)
        target[h, me] = source[h, me]

        def done():
            sent, got = source.at[h, 1:owners], target.at[h, 1:owners]
            pltpu.make_async_copy(got, got, recv_sem.at[h]).wait()
            pltpu.make_async_copy(sent, sent, send_sem.at[h]).wait()

        return done

    def make_factor():
        row = lax.broadcasted_iota(jnp.int32, (2 * m * owners // 2, cells), 0)
        mode = me * m + (row & (m - 1))
        u = (mode - lx // 4).astype(jnp.float32) * (2.0 * np.pi / lx)
        v = u * u
        sine = jnp.zeros_like(u)
        cosine = jnp.zeros_like(u)
        for n in range(9, -1, -1):
            sign = -1.0 if n % 2 else 1.0
            sine = sine * v + sign / float(np.prod(np.arange(1.0, 2 * n + 1)))
            cosine = cosine * v + sign / float(np.prod(np.arange(1.0, 2 * n + 2)))
        cosine = -u * cosine
        kx = (
            1.5 * sine - 0.6 * sine * cosine + sine * (3.0 - 4.0 * sine * sine) * (1.0 / 30.0)
        )
        zero_mode = mode == 0
        kx = jnp.where(zero_mode, 0.0, kx)
        ky, kz = plane[2], plane[3]
        symbol = jnp.zeros_like(kx)
        for c in range(3):
            mixed = metric[c, 0] * kx + metric[c, 1] * ky + metric[c, 2] * kz
            symbol = symbol + mixed * mixed
        at_edge = zero_mode & (plane[4] > 0.5)
        total = float(lx * ey * gy * ez * gz)
        factor[...] = jnp.where(at_edge, 0.0, -1.0 / (jnp.where(at_edge, 1.0, symbol) * total))

    pending = []
    for h in range(parts):
        for copy in f_side[h]:
            copy.wait()
        if h == 0:
            f_top.wait()
        if h == last:
            f_low.wait()
        lo, hi = h * part, (h + 1) * part
        e = split(halo_f[h])
        d = split((div[lo:hi] + dot(beside_sum[h], e[0]) + dot(beside_sum[h], e[1])) * sixtieth)
        line[:, lo:hi] = dot3((big[0], big[1]), d, 1, 1)
        spread(there, h)
        pending.append(exchange(there, here, a_send, a_recv, h))
    make_factor()
    for done in pending:
        done()

    half = lx // 2
    out = dot3((big[4], big[5]), split(jnp.concatenate([gather(here, h) for h in range(parts)], axis=1)))
    re, im = out[:half], out[half:]
    tr, ti = plane[0], plane[1]
    both = jnp.concatenate([re * tr - im * ti, re * ti + im * tr], axis=1)
    out = dot3(split(both), (big[8], big[9]))
    re, im = out[:, :cells] * factor[...], out[:, cells:] * factor[...]
    both = jnp.concatenate([re, im], axis=1)
    out = dot3(split(both), (big[10], big[11]))
    re, im = out[:, :cells], out[:, cells:]
    both = jnp.concatenate([re * tr + im * ti, im * tr - re * ti], axis=0)
    line[...] = dot3((big[6], big[7]), split(both))
    pending = []
    for h in range(parts):
        spread(there2, h)
        pending.append(exchange(there2, here2, b_send, b_recv, h))
    side_p, low_p, top_p = borders(press, edge_p, halo_p, p_send, p_recv)
    p_side = []
    for h in range(parts):
        pending[h]()
        lo, hi = h * part, (h + 1) * part
        press[lo:hi] = dot3(split(gather(here2, h)), (big[2], big[3]), 0, 0)
        p = split(press[lo:hi], 3)
        edge_p[h] = dot(pick[...], p[0]) + dot(pick[...], p[1]) + dot(pick[...], p[2])
        p_side.append(side_p(h))
        if h == 0:
            p_low = low_p()
    p_top = top_p()
    p = split(press[...], 3)
    grad[0] = dot(own[...], p[0]) + dot(own[...], p[1]) + dot(own[...], p[2])
    grad_x[0] = dot(p[0], along_x[...]) + dot(p[1], along_x[...]) + dot(p[2], along_x[...])
    for h in range(parts):
        for copy in p_side[h]:
            copy.wait()
        if h == 0:
            p_top.wait()
        if h == last:
            p_low.wait()
        lo, hi = h * part, (h + 1) * part
        e = split(halo_p[h], 3)
        more = dot(beside[h], e[0]) + dot(beside[h], e[1]) + dot(beside[h], e[2])
        grad[0, lo:hi] += more[:part]
        grad[0, cells + lo : cells + hi] += more[part:]

    def project(i, carry):
        rows = pl.ds(pl.multiple_of(i * 16, 16), 16)
        rows_z = pl.ds(pl.multiple_of(cells + i * 16, 16), 16)
        push = [
            grad_x[0, rows, :] * sixtieth, grad[0, rows, :] * sixtieth, grad[0, rows_z, :] * sixtieth
        ]
        for c in range(3):
            motion[c, rows, :] = prov[c, rows, :] - (
                metric[c, 0] * push[0] + metric[c, 1] * push[1] + metric[c, 2] * push[2]
            )
        return carry

    lax.fori_loop(0, cells // 16, project, 0)


def shards(flow_state, metric, deformation):
    gy, gz = lax.axis_size("gy"), lax.axis_size("gz")
    owners = gy * gz
    _, ez, ey, lx = flow_state.shape
    cells = ez * ey
    m = lx // 2 // owners
    own, beside, pick, along_x = stencil_tables(ez, ey, lx)
    cos_x, sin_x, weight = x_tables(lx)
    ahead = by_owner(cos_x, sin_x, owners)
    back = by_owner(cos_x * weight, sin_x * weight, owners)
    twist, kron, block, ky, kz, edge = plane_tables(gy, gz, ey, ez)
    eye = np.eye(m)
    br, bi = np.cos(block), np.sin(block)
    pair = np.stack([np.stack([br, -bi], 1), np.stack([bi, br], 1)], 0)
    across = np.einsum("atsb,mn->atmsbn", pair.transpose(0, 1, 3, 2), eye)
    across = across.reshape(lx, lx)
    wr, wi = np.cos(kron), np.sin(kron)
    within = np.block([[wr, wi], [-wi, wr]])
    big = np.stack(
        halves(ahead) + halves(back) + halves(across) + halves(across.T)
        + halves(within) + halves(within.T)
    )
    plane = np.repeat(
        np.stack([np.cos(twist), np.sin(twist), ky, kz, edge.astype(np.float64)]), m, axis=1
    ).astype(np.float32)
    bf = jnp.bfloat16
    f32 = jnp.float32
    vmem = pl.BlockSpec(memory_space=pltpu.VMEM)
    smem = pl.BlockSpec(memory_space=pltpu.SMEM)
    hbm = pl.BlockSpec(memory_space=pl.ANY)
    zc = ez // parts
    wide = 6 * zc + 4 * ey
    part = zc * ey
    dma = pltpu.SemaphoreType.DMA
    motion, heat_next = pl.pallas_call(
        lambda *refs: kernel((gy, gz, ez, ey, lx), *refs),
        out_shape=(
            jax.ShapeDtypeStruct((3, cells, lx), f32), jax.ShapeDtypeStruct((cells, lx), f32)
        ),
        in_specs=[smem, smem] + [vmem] * 6 + [hbm] * 2,
        out_specs=(vmem, vmem),
        scratch_shapes=[
            pltpu.VMEM(big.shape, bf),
            pltpu.VMEM(plane.shape, f32),
            pltpu.VMEM((parts, 2, 4, 3 * zc, lx), bf),
            pltpu.VMEM((parts, 4, wide, lx), bf),
            pltpu.VMEM((4, 2 * cells, lx), f32),
            pltpu.VMEM((4, cells, lx), f32),
            pltpu.VMEM((3, cells, lx), f32),
            pltpu.VMEM((3, cells, lx), f32),
            pltpu.VMEM((parts, 6 * zc, lx), f32),
            pltpu.VMEM((parts, wide, lx), f32),
            pltpu.VMEM((cells, lx), f32),
            pltpu.VMEM((parts, 6 * zc, lx), f32),
            pltpu.VMEM((parts, wide, lx), f32),
            pltpu.VMEM((cells, lx), f32),
            pltpu.VMEM((lx, cells), f32),
        ]
        + [pltpu.VMEM((parts, owners, 2 * m, part), f32)] * 4
        + [pltpu.VMEM((lx // 2, cells), f32)]
        + [dma((2,))] + [dma((2 * parts + 2,))] * 6 + [dma((parts,))] * 4,
        compiler_params=pltpu.CompilerParams(
            collective_id=0, has_side_effects=True, vmem_limit_bytes=56 * 2**20
        ),
        cost_estimate=pl.CostEstimate(
            flops=4 * 10**9, bytes_accessed=12 * 2**20, transcendentals=0
        ),
        name="substep",
    )(
        metric, deformation, flow_state.reshape(4, cells, lx),
        jnp.asarray(own, bf), jnp.asarray(beside, bf),
        jnp.asarray(beside[:, :part] + beside[:, part:], bf), jnp.asarray(pick, bf),
        jnp.asarray(along_x, bf), jnp.asarray(big), jnp.asarray(plane),
    )
    return motion.reshape(3, ez, ey, lx), heat_next.reshape(ez, ey, lx)

def solution(mesh):
    placed = (P(None, "gz", "gy", None), P(), P())
    return jax.shard_map(
        shards,
        mesh=mesh,
        in_specs=placed,
        out_specs=(P(None, "gz", "gy", None), P("gz", "gy", None)),
        check_vma=False,
    )
```

```python
import numpy as np

import jax
import jax.numpy as jnp
from jax import lax
from jax.experimental import pallas as pl
from jax.experimental.pallas import tpu as pltpu
from jax.sharding import PartitionSpec as P

substep_width = 0.4
parts = 2
mesh_ids = pl.DeviceIdType.MESH
coefs = {1: 45.0, 2: -9.0, 3: 1.0, -1: -45.0, -2: 9.0, -3: -1.0}


def x_tables(length):
    half = length // 2
    k = np.arange(half)[:, None]
    x = np.arange(length)[None, :]
    angle = 2.0 * np.pi * ((k * x) % length) / length
    c, s = np.cos(angle), -np.sin(angle)
    s[0] = np.where(np.arange(length) % 2 == 0, 1.0, -1.0)
    weight = np.where(np.arange(half) == 0, 1.0, 2.0)[:, None]
    return c, s, weight


def by_owner(re, im, owners):
    half, length = re.shape
    m = half // owners
    return np.concatenate(
        [re.reshape(owners, m, length), im.reshape(owners, m, length)], axis=1
    ).reshape(2 * half, length)


def wave(m, length):
    a = 2.0 * np.pi * m / length
    value = 1.5 * np.sin(a) - 0.3 * np.sin(2 * a) + np.sin(3 * a) / 30.0
    return np.where((2 * m) % length == 0, 0.0, value)


def plane_tables(gy, gz, ey, ez):
    ly, lz = gy * ey, gz * ez
    b = np.repeat(np.arange(ez), ey)
    e = np.tile(np.arange(ey), ez)
    s = np.repeat(np.arange(gy), gz)[:, None]
    q = np.tile(np.arange(gz), gy)[:, None]
    twist = -2.0 * np.pi * (b * q / lz + e * s / ly)
    kron = -2.0 * np.pi * (np.outer(b, b) / ez + np.outer(e, e) / ey)
    my = gy * e[None, :] + s
    mz = gz * b[None, :] + q
    block = -2.0 * np.pi * (
        np.outer(s, s) / gy + np.outer(q, q) / gz
    )
    edge = ((2 * my) % ly == 0) & ((2 * mz) % lz == 0)
    return twist, kron, block, wave(my, ly), wave(mz, lz), edge


def stencil_tables(ez, ey, lx):
    cells, zc = ez * ey, ez // parts
    part = zc * ey
    own = np.zeros((2 * cells, cells))
    beside = np.zeros((parts, 2 * part, 6 * zc + 4 * ey))
    pick = np.zeros((6 * zc, part))
    for z in range(ez):
        h, zh = z // zc, z % zc
        for y in range(ey):
            r, rh = z * ey + y, zh * ey + y
            for o, w in coefs.items():
                t = y + o
                if 0 <= t < ey:
                    own[r, z * ey + t] += w
                elif t < 0:
                    beside[h, rh, (t + 3) * zc + zh] += w
                else:
                    beside[h, rh, (3 + t - ey) * zc + zh] += w
                t = z + o
                if 0 <= t < ez:
                    own[cells + r, t * ey + y] += w
                elif t < 0:
                    beside[h, part + rh, 6 * zc + (t + 4) * ey + y] += w
                else:
                    beside[h, part + rh, 6 * zc + (t - ez) * ey + y] += w
        for j in range(3):
            pick[j * zc + zh, zh * ey + ey - 3 + j] = 1.0
            pick[(3 + j) * zc + zh, zh * ey + j] = 1.0
    along_x = np.zeros((lx, lx))
    for o, w in coefs.items():
        x = np.arange(lx)
        along_x[(x + o) % lx, x] += w
    return own, beside, pick, along_x


def halves(a):
    a = np.asarray(a, np.float32)
    top = a.astype(jnp.bfloat16)
    return [top, (a - top.astype(np.float32)).astype(jnp.bfloat16)]


def split(x, pieces=2):
    out = []
    for _ in range(pieces):
        top = x.astype(jnp.bfloat16)
        out.append(top)
        x = x - top.astype(jnp.float32)
    return out


code_top = 2.0**7.5


def encode(x):
    top = jnp.maximum(jnp.max(jnp.abs(x), axis=0, keepdims=True), 1e-30)
    t = x * (code_top / top)
    for _ in range(4):
        t = t * t
    return jnp.where(x < 0.0, -t, t), top


def decode(code, top):
    code = code.astype(jnp.float32)
    size = jnp.abs(code)
    root = jnp.exp(jnp.log(jnp.maximum(size, 1e-37)) * (1.0 / 16.0)) * (top * (1.0 / code_top))
    root = jnp.where(size < 1e-37, 0.0, root)
    return jnp.where(code < 0.0, -root, root)


def dot(a, b, ca=1, cb=0):
    return lax.dot_general(a, b, (((ca,), (cb,)), ((), ())), preferred_element_type=jnp.float32)


def dot3(a, b, ca=1, cb=0):
    return dot(a[0], b[0], ca, cb) + dot(a[0], b[1], ca, cb) + dot(a[1], b[0], ca, cb)


def kernel(
    sizes, metric, deform, state, own, beside, beside_sum, pick, along_x, big_hbm, plane_hbm,
    motion, heat_next,
    big, plane, edge_state, halo_state, grad, grad_x, prov, flux, edge_f, halo_f, div, code_f, code_halo_f, top_f, top_halo_f, tops, top_line,
    edge_p, halo_p, press, line, there, here, there2, here2, factor,
    load_sem, t_send, t_recv, u_send, u_recv, s_send, s_recv, f_send, f_recv, p_send, p_recv, a_send, a_recv, b_send, b_recv,
):
    gy, gz, ez, ey, lx = sizes
    owners = gy * gz
    cells = ez * ey
    rows2 = lx // owners
    m = rows2 // 2
    zc = ez // parts
    part = zc * ey
    ye, ze = 3 * zc, 4 * ey
    last = parts - 1
    iy, iz = lax.axis_index("gy"), lax.axis_index("gz")
    me = iy * gz + iz
    up_y = (lax.rem(iy + 1, gy), iz)
    down_y = (lax.rem(iy + gy - 1, gy), iz)
    up_z = (iy, lax.rem(iz + 1, gz))
    down_z = (iy, lax.rem(iz + gz - 1, gz))

    load_big = pltpu.make_async_copy(big_hbm, big, load_sem.at[0])
    load_plane = pltpu.make_async_copy(plane_hbm, plane, load_sem.at[1])
    load_big.start()
    load_plane.start()

    def to_all(begin):
        for dz in range(1, gz):
            begin(iy, lax.rem(iz + dz, gz))

        def ring(dy, carry):
            oy = lax.rem(iy + dy, gy)
            for dz in range(gz):
                begin(oy, lax.rem(iz + dz, gz))
            return carry

        lax.fori_loop(1, gy, ring, 0)

    barrier = pltpu.get_barrier_semaphore()

    def greet(oy, oz):
        pl.semaphore_signal(barrier, inc=1, device_id=(oy, oz), device_id_type=mesh_ids)

    to_all(greet)

    for h in range(parts):
        for c in range(4):
            picked = dot(pick[...], state[c, h * part : (h + 1) * part]).astype(jnp.bfloat16)
            edge_state[h, 0, c] = picked[:ye]
            edge_state[h, 1, c] = picked[ye:]
    pl.semaphore_wait(barrier, owners - 1)

    def send(src, dst, send_sem, recv_sem, to):
        copy = pltpu.make_async_remote_copy(
            src_ref=src, dst_ref=dst, send_sem=send_sem, recv_sem=recv_sem,
            device_id=to, device_id_type=mesh_ids,
        )
        copy.start()
        return copy

    side_z = [
        send(
            state.at[:, cells - ze : cells], halo_state.at[0, :, 2 * ye : 2 * ye + ze],
            s_send.at[2 * parts], s_recv.at[2 * parts], up_z,
        ),
        send(
            state.at[:, 0:ze], halo_state.at[last, :, 2 * ye : 2 * ye + ze],
            s_send.at[2 * parts + 1], s_recv.at[2 * parts + 1], down_z,
        ),
    ]
    side_y = [
        [
            send(
                edge_state.at[h, w], halo_state.at[h, :, w * ye : (w + 1) * ye],
                s_send.at[2 * h + w], s_recv.at[2 * h + w], (up_y, down_y)[w],
            )
            for w in range(2)
        ]
        for h in range(parts)
    ]
    for c in range(4):
        grad[c] = dot(own[...], state[c])
        grad_x[c] = dot(state[c], along_x[...])

    def borders(field, edges, halo, sends, recvs):
        def side(h, edges=edges, halo=halo):
            return [
                send(
                    edges.at[h, w * ye : (w + 1) * ye], halo.at[h, w * ye : (w + 1) * ye],
                    sends.at[2 * h + w], recvs.at[2 * h + w], (up_y, down_y)[w],
                )
                for w in range(2)
            ]

        def low():
            return send(
                field.at[0:ze], halo.at[last, 2 * ye : 2 * ye + ze],
                sends.at[2 * parts + 1], recvs.at[2 * parts + 1], down_z,
            )

        def top():
            return send(
                field.at[cells - ze : cells], halo.at[0, 2 * ye : 2 * ye + ze],
                sends.at[2 * parts], recvs.at[2 * parts], up_z,
            )

        return side, low, top

    sixtieth = 1.0 / 60.0

    def advance(i, carry):
        rows = pl.ds(pl.multiple_of(i * 16, 16), 16)
        rows_z = pl.ds(pl.multiple_of(cells + i * 16, 16), 16)
        f = [state[c, rows, :].astype(jnp.float32) for c in range(4)]
        contra = [
            (metric[0, j] * f[0] + metric[1, j] * f[1] + metric[2, j] * f[2]) * sixtieth
            for j in range(3)
        ]
        carried = [
            contra[0] * grad_x[c, rows, :]
            + contra[1] * grad[c, rows, :]
            + contra[2] * grad[c, rows_z, :]
            for c in range(4)
        ]
        new = []
        for c in range(3):
            change = -carried[c] - (
                deform[c, 0] * f[0] + deform[c, 1] * f[1] + deform[c, 2] * f[2]
            )
            if c == 2:
                change = change + f[3]
            new.append(f[c] + substep_width * change)
            prov[c, rows, :] = new[c]
        heat_next[rows, :] = f[3] + substep_width * (-carried[3] - f[2])
        for j in range(3):
            flux[j, rows, :] = metric[0, j] * new[0] + metric[1, j] * new[1] + metric[2, j] * new[2]
        return carry

    side_f, low_f, high_f = borders(flux.at[2], edge_f, halo_f, f_send, f_recv)
    f_side = []
    for h in range(parts):
        for copy in side_y[h]:
            copy.wait()
        if h == 0:
            for copy in side_z:
                copy.wait()
        lo, hi = h * part, (h + 1) * part
        for c in range(4):
            more = dot(beside[h], halo_state[h, c])
            grad[c, lo:hi] += more[:part]
            grad[c, cells + lo : cells + hi] += more[part:]
        lax.fori_loop(lo // 16, hi // 16, advance, 0)
        f1 = split(flux[1, lo:hi])
        code, top = encode(dot(pick[...], f1[0]) + dot(pick[...], f1[1]))
        code_f[h] = code.astype(jnp.bfloat16)
        top_f[h] = top
        f_side.append(
            side_f(h, code_f, code_halo_f)
            + [
                send(
                    top_f.at[h], top_halo_f.at[h, w], t_send.at[2 * h + w], t_recv.at[2 * h + w],
                    (up_y, down_y)[w],
                )
                for w in range(2)
            ]
        )
        if h == 0:
            f_low = low_f()
    f_top = high_f()

    f0 = split(flux[0])
    f1 = split(flux[1])
    f2 = split(flux[2])
    div[...] = (
        dot(f0[0], along_x[...]) + dot(f0[1], along_x[...])
        + dot(own[0:cells], f1[0]) + dot(own[0:cells], f1[1])
        + dot(own[cells:], f2[0]) + dot(own[cells:], f2[1])
    )
    load_big.wait()
    load_plane.wait()

    def spread(buffer, h):
        lanes = slice(h * part, (h + 1) * part)
        if rows2 % 8 == 0:
            buffer[h] = line[:, lanes].reshape(owners, rows2, part).astype(buffer.dtype)
        else:
            for k in range(owners):
                buffer[h, k] = line[k * rows2 : (k + 1) * rows2, lanes].astype(buffer.dtype)

    def gather(buffer, h):
        if rows2 % 8 == 0:
            return buffer.reshape(owners * rows2, part)
        lanes = slice(h * part, (h + 1) * part)
        for k in range(owners):
            line[k * rows2 : (k + 1) * rows2, lanes] = buffer[k]
        return line[:, lanes]

    def exchange(source, target, send_sem, recv_sem, h, shared=False):
        def begin(oy, oz):
            src = source.at[h, 0] if shared else source.at[h, oy * gz + oz]
            pltpu.make_async_remote_copy(
                src_ref=src, dst_ref=target.at[h, me],
                send_sem=send_sem.at[h], recv_sem=recv_sem.at[h],
                device_id=(oy, oz), device_id_type=mesh_ids,
            ).start()

        to_all(begin)
        target[h, me] = source[h, 0] if shared else source[h, me]

        def done():
            got = target.at[h, 1:owners]
            sent = got if shared else source.at[h, 1:owners]
            pltpu.make_async_copy(got, got, recv_sem.at[h]).wait()
            pltpu.make_async_copy(sent, sent, send_sem.at[h]).wait()

        return done

    def share(source, target, send_sem, recv_sem, h):
        return exchange(source, target, send_sem, recv_sem, h, True)

    def make_factor():
        row = lax.broadcasted_iota(jnp.int32, (2 * m * owners // 2, cells), 0)
        mode = me * m + (row & (m - 1))
        u = (mode - lx // 4).astype(jnp.float32) * (2.0 * np.pi / lx)
        v = u * u
        sine = jnp.zeros_like(u)
        cosine = jnp.zeros_like(u)
        for n in range(9, -1, -1):
            sign = -1.0 if n % 2 else 1.0
            sine = sine * v + sign / float(np.prod(np.arange(1.0, 2 * n + 1)))
            cosine = cosine * v + sign / float(np.prod(np.arange(1.0, 2 * n + 2)))
        cosine = -u * cosine
        kx = (
            1.5 * sine - 0.6 * sine * cosine + sine * (3.0 - 4.0 * sine * sine) * (1.0 / 30.0)
        )
        zero_mode = mode == 0
        kx = jnp.where(zero_mode, 0.0, kx)
        ky, kz = plane[2], plane[3]
        symbol = jnp.zeros_like(kx)
        for c in range(3):
            mixed = metric[c, 0] * kx + metric[c, 1] * ky + metric[c, 2] * kz
            symbol = symbol + mixed * mixed
        at_edge = zero_mode & (plane[4] > 0.5)
        total = float(lx * ey * gy * ez * gz)
        factor[...] = jnp.where(at_edge, 0.0, -1.0 / (jnp.where(at_edge, 1.0, symbol) * total))

    pending = []
    for h in range(parts):
        for copy in f_side[h]:
            copy.wait()
        if h == 0:
            f_top.wait()
        if h == last:
            f_low.wait()
        lo, hi = h * part, (h + 1) * part
        for w in range(2):
            rows = slice(w * ye, (w + 1) * ye)
            halo_f[h, rows] = decode(code_halo_f[h, rows], top_halo_f[h, w])
        e = split(halo_f[h])
        d = split((div[lo:hi] + dot(beside_sum[h], e[0]) + dot(beside_sum[h], e[1])) * sixtieth)
        code, top = encode(dot3((big[0], big[1]), d, 1, 1))
        line[:, lo:hi] = code
        top_line[h, 0] = top
        spread(there, h)
        pending.append(exchange(there, here, a_send, a_recv, h))
        pending.append(share(top_line, tops, u_send, u_recv, h))
    make_factor()
    for done in pending:
        done()

    def received(h):
        return gather(decode(here[h], tops[h]), h)


    half = lx // 2
    out = dot3((big[4], big[5]), split(jnp.concatenate([received(h) for h in range(parts)], axis=1)))
    re, im = out[:half], out[half:]
    tr, ti = plane[0], plane[1]
    both = jnp.concatenate([re * tr - im * ti, re * ti + im * tr], axis=1)
    out = dot3(split(both), (big[8], big[9]))
    re, im = out[:, :cells] * factor[...], out[:, cells:] * factor[...]
    both = jnp.concatenate([re, im], axis=1)
    out = dot3(split(both), (big[10], big[11]))
    re, im = out[:, :cells], out[:, cells:]
    both = jnp.concatenate([re * tr + im * ti, im * tr - re * ti], axis=0)
    line[...] = dot3((big[6], big[7]), split(both))
    pending = []
    for h in range(parts):
        spread(there2, h)
        pending.append(exchange(there2, here2, b_send, b_recv, h))
    side_p, low_p, top_p = borders(press, edge_p, halo_p, p_send, p_recv)
    p_side = []
    for h in range(parts):
        pending[h]()
        lo, hi = h * part, (h + 1) * part
        press[lo:hi] = dot3(split(gather(here2[h], h)), (big[2], big[3]), 0, 0)
        p = split(press[lo:hi], 3)
        edge_p[h] = dot(pick[...], p[0]) + dot(pick[...], p[1]) + dot(pick[...], p[2])
        p_side.append(side_p(h))
        if h == 0:
            p_low = low_p()
    p_top = top_p()
    p = split(press[...], 3)
    grad[0] = dot(own[...], p[0]) + dot(own[...], p[1]) + dot(own[...], p[2])
    grad_x[0] = dot(p[0], along_x[...]) + dot(p[1], along_x[...]) + dot(p[2], along_x[...])
    for h in range(parts):
        for copy in p_side[h]:
            copy.wait()
        if h == 0:
            p_top.wait()
        if h == last:
            p_low.wait()
        lo, hi = h * part, (h + 1) * part
        e = split(halo_p[h], 3)
        more = dot(beside[h], e[0]) + dot(beside[h], e[1]) + dot(beside[h], e[2])
        grad[0, lo:hi] += more[:part]
        grad[0, cells + lo : cells + hi] += more[part:]

    def project(i, carry):
        rows = pl.ds(pl.multiple_of(i * 16, 16), 16)
        rows_z = pl.ds(pl.multiple_of(cells + i * 16, 16), 16)
        push = [
            grad_x[0, rows, :] * sixtieth, grad[0, rows, :] * sixtieth, grad[0, rows_z, :] * sixtieth
        ]
        for c in range(3):
            motion[c, rows, :] = prov[c, rows, :] - (
                metric[c, 0] * push[0] + metric[c, 1] * push[1] + metric[c, 2] * push[2]
            )
        return carry

    lax.fori_loop(0, cells // 16, project, 0)


def shards(flow_state, metric, deformation):
    gy, gz = lax.axis_size("gy"), lax.axis_size("gz")
    owners = gy * gz
    _, ez, ey, lx = flow_state.shape
    cells = ez * ey
    m = lx // 2 // owners
    own, beside, pick, along_x = stencil_tables(ez, ey, lx)
    cos_x, sin_x, weight = x_tables(lx)
    ahead = by_owner(cos_x, sin_x, owners)
    back = by_owner(cos_x * weight, sin_x * weight, owners)
    twist, kron, block, ky, kz, edge = plane_tables(gy, gz, ey, ez)
    eye = np.eye(m)
    br, bi = np.cos(block), np.sin(block)
    pair = np.stack([np.stack([br, -bi], 1), np.stack([bi, br], 1)], 0)
    across = np.einsum("atsb,mn->atmsbn", pair.transpose(0, 1, 3, 2), eye)
    across = across.reshape(lx, lx)
    wr, wi = np.cos(kron), np.sin(kron)
    within = np.block([[wr, wi], [-wi, wr]])
    big = np.stack(
        halves(ahead) + halves(back) + halves(across) + halves(across.T)
        + halves(within) + halves(within.T)
    )
    plane = np.repeat(
        np.stack([np.cos(twist), np.sin(twist), ky, kz, edge.astype(np.float64)]), m, axis=1
    ).astype(np.float32)
    bf = jnp.bfloat16
    f32 = jnp.float32
    vmem = pl.BlockSpec(memory_space=pltpu.VMEM)
    smem = pl.BlockSpec(memory_space=pltpu.SMEM)
    hbm = pl.BlockSpec(memory_space=pl.ANY)
    zc = ez // parts
    wide = 6 * zc + 4 * ey
    part = zc * ey
    dma = pltpu.SemaphoreType.DMA
    motion, heat_next = pl.pallas_call(
        lambda *refs: kernel((gy, gz, ez, ey, lx), *refs),
        out_shape=(
            jax.ShapeDtypeStruct((3, cells, lx), f32), jax.ShapeDtypeStruct((cells, lx), f32)
        ),
        in_specs=[smem, smem] + [vmem] * 6 + [hbm] * 2,
        out_specs=(vmem, vmem),
        scratch_shapes=[
            pltpu.VMEM(big.shape, bf),
            pltpu.VMEM(plane.shape, f32),
            pltpu.VMEM((parts, 2, 4, 3 * zc, lx), bf),
            pltpu.VMEM((parts, 4, wide, lx), bf),
            pltpu.VMEM((4, 2 * cells, lx), f32),
            pltpu.VMEM((4, cells, lx), f32),
            pltpu.VMEM((3, cells, lx), f32),
            pltpu.VMEM((3, cells, lx), f32),
            pltpu.VMEM((parts, 6 * zc, lx), f32),
            pltpu.VMEM((parts, wide, lx), f32),
            pltpu.VMEM((cells, lx), f32),
            pltpu.VMEM((parts, 6 * zc, lx), bf),
            pltpu.VMEM((parts, 6 * zc, lx), bf),
            pltpu.VMEM((parts, 1, lx), f32),
            pltpu.VMEM((parts, 2, 1, lx), f32),
            pltpu.VMEM((parts, owners, 1, part), f32),
            pltpu.VMEM((parts, 1, 1, part), f32),
            pltpu.VMEM((parts, 6 * zc, lx), f32),
            pltpu.VMEM((parts, wide, lx), f32),
            pltpu.VMEM((cells, lx), f32),
            pltpu.VMEM((lx, cells), f32),
        ]
        + [pltpu.VMEM((parts, owners, 2 * m, part), bf)] * 2
        + [pltpu.VMEM((parts, owners, 2 * m, part), f32)] * 2
        + [pltpu.VMEM((lx // 2, cells), f32)]
        + [dma((2,))] + [dma((2 * parts,))] * 2 + [dma((parts,))] * 2 + [dma((2 * parts + 2,))] * 6 + [dma((parts,))] * 4,
        compiler_params=pltpu.CompilerParams(
            collective_id=0, has_side_effects=True, vmem_limit_bytes=56 * 2**20
        ),
        cost_estimate=pl.CostEstimate(
            flops=4 * 10**9, bytes_accessed=12 * 2**20, transcendentals=0
        ),
        name="substep",
    )(
        metric, deformation, flow_state.reshape(4, cells, lx),
        jnp.asarray(own, bf), jnp.asarray(beside, bf),
        jnp.asarray(beside[:, :part] + beside[:, part:], bf), jnp.asarray(pick, bf),
        jnp.asarray(along_x, bf), jnp.asarray(big), jnp.asarray(plane),
    )
    return motion.reshape(3, ez, ey, lx), heat_next.reshape(ez, ey, lx)

def solution(mesh):
    placed = (P(None, "gz", "gy", None), P(), P())
    return jax.shard_map(
        shards,
        mesh=mesh,
        in_specs=placed,
        out_specs=(P(None, "gz", "gy", None), P("gz", "gy", None)),
        check_vma=False,
    )
```

```python
import numpy as np

import jax
import jax.numpy as jnp
from jax import lax
from jax.experimental import pallas as pl
from jax.experimental.pallas import tpu as pltpu
from jax.sharding import PartitionSpec as P

substep_width = 0.4
parts = 2
mesh_ids = pl.DeviceIdType.MESH
coefs = {1: 45.0, 2: -9.0, 3: 1.0, -1: -45.0, -2: 9.0, -3: -1.0}


def x_tables(length):
    half = length // 2
    k = np.arange(half)[:, None]
    x = np.arange(length)[None, :]
    angle = 2.0 * np.pi * ((k * x) % length) / length
    c, s = np.cos(angle), -np.sin(angle)
    s[0] = np.where(np.arange(length) % 2 == 0, 1.0, -1.0)
    weight = np.where(np.arange(half) == 0, 1.0, 2.0)[:, None]
    return c, s, weight


def by_owner(re, im, owners):
    half, length = re.shape
    m = half // owners
    return np.concatenate(
        [re.reshape(owners, m, length), im.reshape(owners, m, length)], axis=1
    ).reshape(2 * half, length)


def wave(m, length):
    a = 2.0 * np.pi * m / length
    value = 1.5 * np.sin(a) - 0.3 * np.sin(2 * a) + np.sin(3 * a) / 30.0
    return np.where((2 * m) % length == 0, 0.0, value)


def plane_tables(gy, gz, ey, ez):
    ly, lz = gy * ey, gz * ez
    b = np.repeat(np.arange(ez), ey)
    e = np.tile(np.arange(ey), ez)
    s = np.repeat(np.arange(gy), gz)[:, None]
    q = np.tile(np.arange(gz), gy)[:, None]
    twist = -2.0 * np.pi * (b * q / lz + e * s / ly)
    kron = -2.0 * np.pi * (np.outer(b, b) / ez + np.outer(e, e) / ey)
    my = gy * e[None, :] + s
    mz = gz * b[None, :] + q
    block = -2.0 * np.pi * (
        np.outer(s, s) / gy + np.outer(q, q) / gz
    )
    edge = ((2 * my) % ly == 0) & ((2 * mz) % lz == 0)
    return twist, kron, block, wave(my, ly), wave(mz, lz), edge


def stencil_tables(ez, ey, lx):
    cells, zc = ez * ey, ez // parts
    part = zc * ey
    own = np.zeros((2 * cells, cells))
    beside = np.zeros((parts, 2 * part, 6 * zc + 4 * ey))
    pick = np.zeros((6 * zc, part))
    for z in range(ez):
        h, zh = z // zc, z % zc
        for y in range(ey):
            r, rh = z * ey + y, zh * ey + y
            for o, w in coefs.items():
                t = y + o
                if 0 <= t < ey:
                    own[r, z * ey + t] += w
                elif t < 0:
                    beside[h, rh, (t + 3) * zc + zh] += w
                else:
                    beside[h, rh, (3 + t - ey) * zc + zh] += w
                t = z + o
                if 0 <= t < ez:
                    own[cells + r, t * ey + y] += w
                elif t < 0:
                    beside[h, part + rh, 6 * zc + (t + 4) * ey + y] += w
                else:
                    beside[h, part + rh, 6 * zc + (t - ez) * ey + y] += w
        for j in range(3):
            pick[j * zc + zh, zh * ey + ey - 3 + j] = 1.0
            pick[(3 + j) * zc + zh, zh * ey + j] = 1.0
    along_x = np.zeros((lx, lx))
    for o, w in coefs.items():
        x = np.arange(lx)
        along_x[(x + o) % lx, x] += w
    return own, beside, pick, along_x


def halves(a):
    a = np.asarray(a, np.float32)
    top = a.astype(jnp.bfloat16)
    return [top, (a - top.astype(np.float32)).astype(jnp.bfloat16)]


def split(x, pieces=2):
    out = []
    for _ in range(pieces):
        top = x.astype(jnp.bfloat16)
        out.append(top)
        x = x - top.astype(jnp.float32)
    return out


code_top = 2.0**7.5


def encode(x):
    top = jnp.maximum(jnp.max(jnp.abs(x), axis=0, keepdims=True), 1e-30)
    t = x * (code_top / top)
    for _ in range(4):
        t = t * t
    return jnp.where(x < 0.0, -t, t), top


def decode(code, top):
    code = code.astype(jnp.float32)
    size = jnp.abs(code)
    root = jnp.exp(jnp.log(jnp.maximum(size, 1e-37)) * (1.0 / 16.0)) * (top * (1.0 / code_top))
    root = jnp.where(size < 1e-37, 0.0, root)
    return jnp.where(code < 0.0, -root, root)


def dot(a, b, ca=1, cb=0):
    return lax.dot_general(a, b, (((ca,), (cb,)), ((), ())), preferred_element_type=jnp.float32)


def dot3(a, b, ca=1, cb=0):
    return dot(a[0], b[0], ca, cb) + dot(a[0], b[1], ca, cb) + dot(a[1], b[0], ca, cb)


def kernel(
    sizes, metric, deform, state, own, beside, beside_sum, pick, along_x, big_hbm, plane_hbm,
    motion, heat_next,
    big, plane, edge_state, halo_state, grad, grad_x, prov, flux, edge_f, halo_f, div, code_f, code_halo_f, top_f, top_halo_f, tops, top_line,
    edge_p, halo_p, press, line, there, here, there2, here2, factor,
    load_sem, t_send, t_recv, u_send, u_recv, s_send, s_recv, f_send, f_recv, p_send, p_recv, a_send, a_recv, b_send, b_recv,
):
    gy, gz, ez, ey, lx = sizes
    owners = gy * gz
    cells = ez * ey
    rows2 = lx // owners
    m = rows2 // 2
    zc = ez // parts
    part = zc * ey
    ye, ze = 3 * zc, 4 * ey
    last = parts - 1
    iy, iz = lax.axis_index("gy"), lax.axis_index("gz")
    me = iy * gz + iz
    up_y = (lax.rem(iy + 1, gy), iz)
    down_y = (lax.rem(iy + gy - 1, gy), iz)
    up_z = (iy, lax.rem(iz + 1, gz))
    down_z = (iy, lax.rem(iz + gz - 1, gz))

    load_big = pltpu.make_async_copy(big_hbm, big, load_sem.at[0])
    load_plane = pltpu.make_async_copy(plane_hbm, plane, load_sem.at[1])
    load_big.start()
    load_plane.start()

    def to_all(begin):
        for dz in range(1, gz):
            begin(iy, lax.rem(iz + dz, gz))

        def ring(dy, carry):
            oy = lax.rem(iy + dy, gy)
            for dz in range(gz):
                begin(oy, lax.rem(iz + dz, gz))
            return carry

        lax.fori_loop(1, gy, ring, 0)

    barrier = pltpu.get_barrier_semaphore()

    def greet(oy, oz):
        pl.semaphore_signal(barrier, inc=1, device_id=(oy, oz), device_id_type=mesh_ids)

    to_all(greet)

    for h in range(parts):
        for c in range(4):
            picked = dot(pick[...], state[c, h * part : (h + 1) * part]).astype(jnp.bfloat16)
            edge_state[h, 0, c] = picked[:ye]
            edge_state[h, 1, c] = picked[ye:]
    pl.semaphore_wait(barrier, owners - 1)

    def send(src, dst, send_sem, recv_sem, to):
        copy = pltpu.make_async_remote_copy(
            src_ref=src, dst_ref=dst, send_sem=send_sem, recv_sem=recv_sem,
            device_id=to, device_id_type=mesh_ids,
        )
        copy.start()
        return copy

    side_z = [
        send(
            state.at[:, cells - ze : cells], halo_state.at[0, :, 2 * ye : 2 * ye + ze],
            s_send.at[2 * parts], s_recv.at[2 * parts], up_z,
        ),
        send(
            state.at[:, 0:ze], halo_state.at[last, :, 2 * ye : 2 * ye + ze],
            s_send.at[2 * parts + 1], s_recv.at[2 * parts + 1], down_z,
        ),
    ]
    def side_state(h):
        return [
            send(
                edge_state.at[h, w], halo_state.at[h, :, w * ye : (w + 1) * ye],
                s_send.at[2 * h + w], s_recv.at[2 * h + w], (up_y, down_y)[w],
            )
            for w in range(2)
        ]

    side_y = [side_state(0)]
    for c in range(4):
        grad[c] = dot(own[...], state[c])
        grad_x[c] = dot(state[c], along_x[...])

    def borders(field, edges, halo, sends, recvs):
        def side(h, edges=edges, halo=halo):
            return [
                send(
                    edges.at[h, w * ye : (w + 1) * ye], halo.at[h, w * ye : (w + 1) * ye],
                    sends.at[2 * h + w], recvs.at[2 * h + w], (up_y, down_y)[w],
                )
                for w in range(2)
            ]

        def low():
            return send(
                field.at[0:ze], halo.at[last, 2 * ye : 2 * ye + ze],
                sends.at[2 * parts + 1], recvs.at[2 * parts + 1], down_z,
            )

        def top():
            return send(
                field.at[cells - ze : cells], halo.at[0, 2 * ye : 2 * ye + ze],
                sends.at[2 * parts], recvs.at[2 * parts], up_z,
            )

        return side, low, top

    sixtieth = 1.0 / 60.0

    def advance(i, carry):
        rows = pl.ds(pl.multiple_of(i * 16, 16), 16)
        rows_z = pl.ds(pl.multiple_of(cells + i * 16, 16), 16)
        f = [state[c, rows, :].astype(jnp.float32) for c in range(4)]
        contra = [
            (metric[0, j] * f[0] + metric[1, j] * f[1] + metric[2, j] * f[2]) * sixtieth
            for j in range(3)
        ]
        carried = [
            contra[0] * grad_x[c, rows, :]
            + contra[1] * grad[c, rows, :]
            + contra[2] * grad[c, rows_z, :]
            for c in range(4)
        ]
        new = []
        for c in range(3):
            change = -carried[c] - (
                deform[c, 0] * f[0] + deform[c, 1] * f[1] + deform[c, 2] * f[2]
            )
            if c == 2:
                change = change + f[3]
            new.append(f[c] + substep_width * change)
            prov[c, rows, :] = new[c]
        heat_next[rows, :] = f[3] + substep_width * (-carried[3] - f[2])
        for j in range(3):
            flux[j, rows, :] = metric[0, j] * new[0] + metric[1, j] * new[1] + metric[2, j] * new[2]
        return carry

    side_f, low_f, high_f = borders(flux.at[2], edge_f, halo_f, f_send, f_recv)
    f_side = []
    for h in range(parts):
        for copy in side_y[h]:
            copy.wait_send()
        if h < last:
            side_y.append(side_state(h + 1))
        for copy in side_y[h]:
            copy.wait_recv()
        if h == 0:
            for copy in side_z:
                copy.wait()
        lo, hi = h * part, (h + 1) * part
        for c in range(4):
            more = dot(beside[h], halo_state[h, c])
            grad[c, lo:hi] += more[:part]
            grad[c, cells + lo : cells + hi] += more[part:]
        lax.fori_loop(lo // 16, hi // 16, advance, 0)
        f1 = split(flux[1, lo:hi])
        code, top = encode(dot(pick[...], f1[0]) + dot(pick[...], f1[1]))
        code_f[h] = code.astype(jnp.bfloat16)
        top_f[h] = top
        f_side.append(
            side_f(h, code_f, code_halo_f)
            + [
                send(
                    top_f.at[h], top_halo_f.at[h, w], t_send.at[2 * h + w], t_recv.at[2 * h + w],
                    (up_y, down_y)[w],
                )
                for w in range(2)
            ]
        )
        if h == 0:
            f_low = low_f()
    f_top = high_f()

    f0 = split(flux[0])
    f1 = split(flux[1])
    f2 = split(flux[2])
    div[...] = (
        dot(f0[0], along_x[...]) + dot(f0[1], along_x[...])
        + dot(own[0:cells], f1[0]) + dot(own[0:cells], f1[1])
        + dot(own[cells:], f2[0]) + dot(own[cells:], f2[1])
    )
    load_big.wait()
    load_plane.wait()

    def spread(buffer, h):
        lanes = slice(h * part, (h + 1) * part)
        if rows2 % 8 == 0:
            buffer[h] = line[:, lanes].reshape(owners, rows2, part).astype(buffer.dtype)
        else:
            for k in range(owners):
                buffer[h, k] = line[k * rows2 : (k + 1) * rows2, lanes].astype(buffer.dtype)

    def gather(buffer, h):
        if rows2 % 8 == 0:
            return buffer.reshape(owners * rows2, part)
        lanes = slice(h * part, (h + 1) * part)
        for k in range(owners):
            line[k * rows2 : (k + 1) * rows2, lanes] = buffer[k]
        return line[:, lanes]

    def exchange(source, target, send_sem, recv_sem, h, shared=False):
        def begin(oy, oz):
            src = source.at[h, 0] if shared else source.at[h, oy * gz + oz]
            pltpu.make_async_remote_copy(
                src_ref=src, dst_ref=target.at[h, me],
                send_sem=send_sem.at[h], recv_sem=recv_sem.at[h],
                device_id=(oy, oz), device_id_type=mesh_ids,
            ).start()

        to_all(begin)
        target[h, me] = source[h, 0] if shared else source[h, me]

        def done():
            got = target.at[h, 1:owners]
            sent = got if shared else source.at[h, 1:owners]
            pltpu.make_async_copy(got, got, recv_sem.at[h]).wait()
            pltpu.make_async_copy(sent, sent, send_sem.at[h]).wait()

        return done

    def share(source, target, send_sem, recv_sem, h):
        return exchange(source, target, send_sem, recv_sem, h, True)

    def make_factor():
        row = lax.broadcasted_iota(jnp.int32, (2 * m * owners // 2, cells), 0)
        mode = me * m + (row & (m - 1))
        u = (mode - lx // 4).astype(jnp.float32) * (2.0 * np.pi / lx)
        v = u * u
        sine = jnp.zeros_like(u)
        cosine = jnp.zeros_like(u)
        for n in range(9, -1, -1):
            sign = -1.0 if n % 2 else 1.0
            sine = sine * v + sign / float(np.prod(np.arange(1.0, 2 * n + 1)))
            cosine = cosine * v + sign / float(np.prod(np.arange(1.0, 2 * n + 2)))
        cosine = -u * cosine
        kx = (
            1.5 * sine - 0.6 * sine * cosine + sine * (3.0 - 4.0 * sine * sine) * (1.0 / 30.0)
        )
        zero_mode = mode == 0
        kx = jnp.where(zero_mode, 0.0, kx)
        ky, kz = plane[2], plane[3]
        symbol = jnp.zeros_like(kx)
        for c in range(3):
            mixed = metric[c, 0] * kx + metric[c, 1] * ky + metric[c, 2] * kz
            symbol = symbol + mixed * mixed
        at_edge = zero_mode & (plane[4] > 0.5)
        total = float(lx * ey * gy * ez * gz)
        factor[...] = jnp.where(at_edge, 0.0, -1.0 / (jnp.where(at_edge, 1.0, symbol) * total))

    pending = []
    for h in range(parts):
        for copy in f_side[h]:
            copy.wait()
        if h == 0:
            f_top.wait()
        if h == last:
            f_low.wait()
        lo, hi = h * part, (h + 1) * part
        for w in range(2):
            rows = slice(w * ye, (w + 1) * ye)
            halo_f[h, rows] = decode(code_halo_f[h, rows], top_halo_f[h, w])
        e = split(halo_f[h])
        d = split((div[lo:hi] + dot(beside_sum[h], e[0]) + dot(beside_sum[h], e[1])) * sixtieth)
        code, top = encode(dot3((big[0], big[1]), d, 1, 1))
        line[:, lo:hi] = code
        top_line[h, 0] = top
        spread(there, h)
        pending.append(exchange(there, here, a_send, a_recv, h))
        pending.append(share(top_line, tops, u_send, u_recv, h))
    make_factor()
    for done in pending:
        done()

    def received(h):
        return gather(decode(here[h], tops[h]), h)


    half = lx // 2
    out = dot3((big[4], big[5]), split(jnp.concatenate([received(h) for h in range(parts)], axis=1)))
    re, im = out[:half], out[half:]
    tr, ti = plane[0], plane[1]
    both = jnp.concatenate([re * tr - im * ti, re * ti + im * tr], axis=1)
    out = dot3(split(both), (big[8], big[9]))
    re, im = out[:, :cells] * factor[...], out[:, cells:] * factor[...]
    both = jnp.concatenate([re, im], axis=1)
    out = dot3(split(both), (big[10], big[11]))
    re, im = out[:, :cells], out[:, cells:]
    both = jnp.concatenate([re * tr + im * ti, im * tr - re * ti], axis=0)
    line[...] = dot3((big[6], big[7]), split(both))
    pending = []
    for h in range(parts):
        spread(there2, h)
        pending.append(exchange(there2, here2, b_send, b_recv, h))
    side_p, low_p, top_p = borders(press, edge_p, halo_p, p_send, p_recv)
    p_side = []
    for h in range(parts):
        pending[h]()
        lo, hi = h * part, (h + 1) * part
        press[lo:hi] = dot3(split(gather(here2[h], h)), (big[2], big[3]), 0, 0)
        p = split(press[lo:hi], 3)
        edge_p[h] = dot(pick[...], p[0]) + dot(pick[...], p[1]) + dot(pick[...], p[2])
        p_side.append(side_p(h))
        if h == 0:
            p_low = low_p()
    p_top = top_p()
    p = split(press[...], 3)
    grad[0] = dot(own[...], p[0]) + dot(own[...], p[1]) + dot(own[...], p[2])
    grad_x[0] = dot(p[0], along_x[...]) + dot(p[1], along_x[...]) + dot(p[2], along_x[...])
    for h in range(parts):
        for copy in p_side[h]:
            copy.wait()
        if h == 0:
            p_top.wait()
        if h == last:
            p_low.wait()
        lo, hi = h * part, (h + 1) * part
        e = split(halo_p[h], 3)
        more = dot(beside[h], e[0]) + dot(beside[h], e[1]) + dot(beside[h], e[2])
        grad[0, lo:hi] += more[:part]
        grad[0, cells + lo : cells + hi] += more[part:]

    def project(i, carry):
        rows = pl.ds(pl.multiple_of(i * 16, 16), 16)
        rows_z = pl.ds(pl.multiple_of(cells + i * 16, 16), 16)
        push = [
            grad_x[0, rows, :] * sixtieth, grad[0, rows, :] * sixtieth, grad[0, rows_z, :] * sixtieth
        ]
        for c in range(3):
            motion[c, rows, :] = prov[c, rows, :] - (
                metric[c, 0] * push[0] + metric[c, 1] * push[1] + metric[c, 2] * push[2]
            )
        return carry

    lax.fori_loop(0, cells // 16, project, 0)


def shards(flow_state, metric, deformation):
    gy, gz = lax.axis_size("gy"), lax.axis_size("gz")
    owners = gy * gz
    _, ez, ey, lx = flow_state.shape
    cells = ez * ey
    m = lx // 2 // owners
    own, beside, pick, along_x = stencil_tables(ez, ey, lx)
    cos_x, sin_x, weight = x_tables(lx)
    ahead = by_owner(cos_x, sin_x, owners)
    back = by_owner(cos_x * weight, sin_x * weight, owners)
    twist, kron, block, ky, kz, edge = plane_tables(gy, gz, ey, ez)
    eye = np.eye(m)
    br, bi = np.cos(block), np.sin(block)
    pair = np.stack([np.stack([br, -bi], 1), np.stack([bi, br], 1)], 0)
    across = np.einsum("atsb,mn->atmsbn", pair.transpose(0, 1, 3, 2), eye)
    across = across.reshape(lx, lx)
    wr, wi = np.cos(kron), np.sin(kron)
    within = np.block([[wr, wi], [-wi, wr]])
    big = np.stack(
        halves(ahead) + halves(back) + halves(across) + halves(across.T)
        + halves(within) + halves(within.T)
    )
    plane = np.repeat(
        np.stack([np.cos(twist), np.sin(twist), ky, kz, edge.astype(np.float64)]), m, axis=1
    ).astype(np.float32)
    bf = jnp.bfloat16
    f32 = jnp.float32
    vmem = pl.BlockSpec(memory_space=pltpu.VMEM)
    smem = pl.BlockSpec(memory_space=pltpu.SMEM)
    hbm = pl.BlockSpec(memory_space=pl.ANY)
    zc = ez // parts
    wide = 6 * zc + 4 * ey
    part = zc * ey
    dma = pltpu.SemaphoreType.DMA
    motion, heat_next = pl.pallas_call(
        lambda *refs: kernel((gy, gz, ez, ey, lx), *refs),
        out_shape=(
            jax.ShapeDtypeStruct((3, cells, lx), f32), jax.ShapeDtypeStruct((cells, lx), f32)
        ),
        in_specs=[smem, smem] + [vmem] * 6 + [hbm] * 2,
        out_specs=(vmem, vmem),
        scratch_shapes=[
            pltpu.VMEM(big.shape, bf),
            pltpu.VMEM(plane.shape, f32),
            pltpu.VMEM((parts, 2, 4, 3 * zc, lx), bf),
            pltpu.VMEM((parts, 4, wide, lx), bf),
            pltpu.VMEM((4, 2 * cells, lx), f32),
            pltpu.VMEM((4, cells, lx), f32),
            pltpu.VMEM((3, cells, lx), f32),
            pltpu.VMEM((3, cells, lx), f32),
            pltpu.VMEM((parts, 6 * zc, lx), f32),
            pltpu.VMEM((parts, wide, lx), f32),
            pltpu.VMEM((cells, lx), f32),
            pltpu.VMEM((parts, 6 * zc, lx), bf),
            pltpu.VMEM((parts, 6 * zc, lx), bf),
            pltpu.VMEM((parts, 1, lx), f32),
            pltpu.VMEM((parts, 2, 1, lx), f32),
            pltpu.VMEM((parts, owners, 1, part), f32),
            pltpu.VMEM((parts, 1, 1, part), f32),
            pltpu.VMEM((parts, 6 * zc, lx), f32),
            pltpu.VMEM((parts, wide, lx), f32),
            pltpu.VMEM((cells, lx), f32),
            pltpu.VMEM((lx, cells), f32),
        ]
        + [pltpu.VMEM((parts, owners, 2 * m, part), bf)] * 2
        + [pltpu.VMEM((parts, owners, 2 * m, part), f32)] * 2
        + [pltpu.VMEM((lx // 2, cells), f32)]
        + [dma((2,))] + [dma((2 * parts,))] * 2 + [dma((parts,))] * 2 + [dma((2 * parts + 2,))] * 6 + [dma((parts,))] * 4,
        compiler_params=pltpu.CompilerParams(
            collective_id=0, has_side_effects=True, vmem_limit_bytes=56 * 2**20
        ),
        cost_estimate=pl.CostEstimate(
            flops=4 * 10**9, bytes_accessed=12 * 2**20, transcendentals=0
        ),
        name="substep",
    )(
        metric, deformation, flow_state.reshape(4, cells, lx),
        jnp.asarray(own, bf), jnp.asarray(beside, bf),
        jnp.asarray(beside[:, :part] + beside[:, part:], bf), jnp.asarray(pick, bf),
        jnp.asarray(along_x, bf), jnp.asarray(big), jnp.asarray(plane),
    )
    return motion.reshape(3, ez, ey, lx), heat_next.reshape(ez, ey, lx)

def solution(mesh):
    placed = (P(None, "gz", "gy", None), P(), P())
    return jax.shard_map(
        shards,
        mesh=mesh,
        in_specs=placed,
        out_specs=(P(None, "gz", "gy", None), P("gz", "gy", None)),
        check_vma=False,
    )
```

```python
import numpy as np

import jax
import jax.numpy as jnp
from jax import lax
from jax.experimental import pallas as pl
from jax.experimental.pallas import tpu as pltpu
from jax.sharding import PartitionSpec as P

substep_width = 0.4
parts = 2
mesh_ids = pl.DeviceIdType.MESH
coefs = {1: 45.0, 2: -9.0, 3: 1.0, -1: -45.0, -2: 9.0, -3: -1.0}


def x_tables(length):
    half = length // 2
    k = np.arange(half)[:, None]
    x = np.arange(length)[None, :]
    angle = 2.0 * np.pi * ((k * x) % length) / length
    c, s = np.cos(angle), -np.sin(angle)
    s[0] = np.where(np.arange(length) % 2 == 0, 1.0, -1.0)
    weight = np.where(np.arange(half) == 0, 1.0, 2.0)[:, None]
    return c, s, weight


def by_owner(re, im, owners):
    half, length = re.shape
    m = half // owners
    return np.concatenate(
        [re.reshape(owners, m, length), im.reshape(owners, m, length)], axis=1
    ).reshape(2 * half, length)


def wave(m, length):
    a = 2.0 * np.pi * m / length
    value = 1.5 * np.sin(a) - 0.3 * np.sin(2 * a) + np.sin(3 * a) / 30.0
    return np.where((2 * m) % length == 0, 0.0, value)


def plane_tables(gy, gz, ey, ez):
    ly, lz = gy * ey, gz * ez
    b = np.repeat(np.arange(ez), ey)
    e = np.tile(np.arange(ey), ez)
    s = np.repeat(np.arange(gy), gz)[:, None]
    q = np.tile(np.arange(gz), gy)[:, None]
    twist = -2.0 * np.pi * (b * q / lz + e * s / ly)
    kron = -2.0 * np.pi * (np.outer(b, b) / ez + np.outer(e, e) / ey)
    my = gy * e[None, :] + s
    mz = gz * b[None, :] + q
    block = -2.0 * np.pi * (
        np.outer(s, s) / gy + np.outer(q, q) / gz
    )
    edge = ((2 * my) % ly == 0) & ((2 * mz) % lz == 0)
    return twist, kron, block, wave(my, ly), wave(mz, lz), edge


def stencil_tables(ez, ey, lx):
    cells, zc = ez * ey, ez // parts
    part = zc * ey
    own = np.zeros((2 * cells, cells))
    beside = np.zeros((parts, 2 * part, 6 * zc + 4 * ey))
    pick = np.zeros((6 * zc, part))
    for z in range(ez):
        h, zh = z // zc, z % zc
        for y in range(ey):
            r, rh = z * ey + y, zh * ey + y
            for o, w in coefs.items():
                t = y + o
                if 0 <= t < ey:
                    own[r, z * ey + t] += w
                elif t < 0:
                    beside[h, rh, (t + 3) * zc + zh] += w
                else:
                    beside[h, rh, (3 + t - ey) * zc + zh] += w
                t = z + o
                if 0 <= t < ez:
                    own[cells + r, t * ey + y] += w
                elif t < 0:
                    beside[h, part + rh, 6 * zc + (t + 4) * ey + y] += w
                else:
                    beside[h, part + rh, 6 * zc + (t - ez) * ey + y] += w
        for j in range(3):
            pick[j * zc + zh, zh * ey + ey - 3 + j] = 1.0
            pick[(3 + j) * zc + zh, zh * ey + j] = 1.0
    along_x = np.zeros((lx, lx))
    for o, w in coefs.items():
        x = np.arange(lx)
        along_x[(x + o) % lx, x] += w
    return own, beside, pick, along_x


def halves(a):
    a = np.asarray(a, np.float32)
    top = a.astype(jnp.bfloat16)
    return [top, (a - top.astype(np.float32)).astype(jnp.bfloat16)]


def split(x, pieces=2):
    out = []
    for _ in range(pieces):
        top = x.astype(jnp.bfloat16)
        out.append(top)
        x = x - top.astype(jnp.float32)
    return out


code_top = 2.0**7.5


def encode(x):
    top = jnp.maximum(jnp.max(jnp.abs(x), axis=0, keepdims=True), 1e-30)
    t = x * (code_top / top)
    for _ in range(4):
        t = t * t
    return jnp.where(x < 0.0, -t, t), top


def decode(code, top):
    code = code.astype(jnp.float32)
    size = jnp.abs(code)
    root = jnp.exp(jnp.log(jnp.maximum(size, 1e-37)) * (1.0 / 16.0)) * (top * (1.0 / code_top))
    root = jnp.where(size < 1e-37, 0.0, root)
    return jnp.where(code < 0.0, -root, root)


def dot(a, b, ca=1, cb=0):
    return lax.dot_general(a, b, (((ca,), (cb,)), ((), ())), preferred_element_type=jnp.float32)


def dot3(a, b, ca=1, cb=0):
    return dot(a[0], b[0], ca, cb) + dot(a[0], b[1], ca, cb) + dot(a[1], b[0], ca, cb)


def kernel(
    sizes, metric, deform, state, own, beside, beside_sum, pick, along_x, big_hbm, plane_hbm,
    prov_out, heat_out, push_x_out, push_yz_out,
    heat_next, big, plane, edge_state, halo_state, grad, grad_x, prov, flux, edge_f, halo_f, div, code_f, code_halo_f, top_f, top_halo_f, tops, top_line,
    edge_p, halo_p, press, line, there, here, there2, here2, factor,
    load_sem, out_sem, t_send, t_recv, u_send, u_recv, s_send, s_recv, f_send, f_recv, p_send, p_recv, a_send, a_recv, b_send, b_recv,
):
    gy, gz, ez, ey, lx = sizes
    owners = gy * gz
    cells = ez * ey
    rows2 = lx // owners
    m = rows2 // 2
    zc = ez // parts
    part = zc * ey
    ye, ze = 3 * zc, 4 * ey
    last = parts - 1
    iy, iz = lax.axis_index("gy"), lax.axis_index("gz")
    me = iy * gz + iz
    up_y = (lax.rem(iy + 1, gy), iz)
    down_y = (lax.rem(iy + gy - 1, gy), iz)
    up_z = (iy, lax.rem(iz + 1, gz))
    down_z = (iy, lax.rem(iz + gz - 1, gz))

    load_big = pltpu.make_async_copy(big_hbm, big, load_sem.at[0])
    load_plane = pltpu.make_async_copy(plane_hbm, plane, load_sem.at[1])
    load_big.start()
    load_plane.start()

    def to_all(begin):
        for dz in range(1, gz):
            begin(iy, lax.rem(iz + dz, gz))

        def ring(dy, carry):
            oy = lax.rem(iy + dy, gy)
            for dz in range(gz):
                begin(oy, lax.rem(iz + dz, gz))
            return carry

        lax.fori_loop(1, gy, ring, 0)

    barrier = pltpu.get_barrier_semaphore()

    def greet(oy, oz):
        pl.semaphore_signal(barrier, inc=1, device_id=(oy, oz), device_id_type=mesh_ids)

    to_all(greet)

    for h in range(parts):
        for c in range(4):
            picked = dot(pick[...], state[c, h * part : (h + 1) * part]).astype(jnp.bfloat16)
            edge_state[h, 0, c] = picked[:ye]
            edge_state[h, 1, c] = picked[ye:]
    pl.semaphore_wait(barrier, owners - 1)

    def send(src, dst, send_sem, recv_sem, to):
        copy = pltpu.make_async_remote_copy(
            src_ref=src, dst_ref=dst, send_sem=send_sem, recv_sem=recv_sem,
            device_id=to, device_id_type=mesh_ids,
        )
        copy.start()
        return copy

    side_z = [
        send(
            state.at[:, cells - ze : cells], halo_state.at[0, :, 2 * ye : 2 * ye + ze],
            s_send.at[2 * parts], s_recv.at[2 * parts], up_z,
        ),
        send(
            state.at[:, 0:ze], halo_state.at[last, :, 2 * ye : 2 * ye + ze],
            s_send.at[2 * parts + 1], s_recv.at[2 * parts + 1], down_z,
        ),
    ]
    side_y = [
        [
            send(
                edge_state.at[h, w], halo_state.at[h, :, w * ye : (w + 1) * ye],
                s_send.at[2 * h + w], s_recv.at[2 * h + w], (up_y, down_y)[w],
            )
            for w in range(2)
        ]
        for h in range(parts)
    ]
    for c in range(4):
        grad[c] = dot(own[...], state[c])
        grad_x[c] = dot(state[c], along_x[...])

    def borders(field, edges, halo, sends, recvs):
        def side(h, edges=edges, halo=halo):
            return [
                send(
                    edges.at[h, w * ye : (w + 1) * ye], halo.at[h, w * ye : (w + 1) * ye],
                    sends.at[2 * h + w], recvs.at[2 * h + w], (up_y, down_y)[w],
                )
                for w in range(2)
            ]

        def low():
            return send(
                field.at[0:ze], halo.at[last, 2 * ye : 2 * ye + ze],
                sends.at[2 * parts + 1], recvs.at[2 * parts + 1], down_z,
            )

        def top():
            return send(
                field.at[cells - ze : cells], halo.at[0, 2 * ye : 2 * ye + ze],
                sends.at[2 * parts], recvs.at[2 * parts], up_z,
            )

        return side, low, top

    sixtieth = 1.0 / 60.0

    def advance(i, carry):
        rows = pl.ds(pl.multiple_of(i * 16, 16), 16)
        rows_z = pl.ds(pl.multiple_of(cells + i * 16, 16), 16)
        f = [state[c, rows, :].astype(jnp.float32) for c in range(4)]
        contra = [
            (metric[0, j] * f[0] + metric[1, j] * f[1] + metric[2, j] * f[2]) * sixtieth
            for j in range(3)
        ]
        carried = [
            contra[0] * grad_x[c, rows, :]
            + contra[1] * grad[c, rows, :]
            + contra[2] * grad[c, rows_z, :]
            for c in range(4)
        ]
        new = []
        for c in range(3):
            change = -carried[c] - (
                deform[c, 0] * f[0] + deform[c, 1] * f[1] + deform[c, 2] * f[2]
            )
            if c == 2:
                change = change + f[3]
            new.append(f[c] + substep_width * change)
            prov[c, rows, :] = new[c]
        heat_next[rows, :] = f[3] + substep_width * (-carried[3] - f[2])
        for j in range(3):
            flux[j, rows, :] = metric[0, j] * new[0] + metric[1, j] * new[1] + metric[2, j] * new[2]
        return carry

    side_f, low_f, high_f = borders(flux.at[2], edge_f, halo_f, f_send, f_recv)
    f_side = []
    for h in range(parts):
        for copy in side_y[h]:
            copy.wait()
        if h == 0:
            for copy in side_z:
                copy.wait()
        lo, hi = h * part, (h + 1) * part
        for c in range(4):
            more = dot(beside[h], halo_state[h, c])
            grad[c, lo:hi] += more[:part]
            grad[c, cells + lo : cells + hi] += more[part:]
        lax.fori_loop(lo // 16, hi // 16, advance, 0)
        f1 = split(flux[1, lo:hi])
        code, top = encode(dot(pick[...], f1[0]) + dot(pick[...], f1[1]))
        code_f[h] = code.astype(jnp.bfloat16)
        top_f[h] = top
        f_side.append(
            side_f(h, code_f, code_halo_f)
            + [
                send(
                    top_f.at[h], top_halo_f.at[h, w], t_send.at[2 * h + w], t_recv.at[2 * h + w],
                    (up_y, down_y)[w],
                )
                for w in range(2)
            ]
        )
        if h == 0:
            f_low = low_f()
    f_top = high_f()
    outgoing = [
        pltpu.make_async_copy(prov, prov_out, out_sem.at[0]),
        pltpu.make_async_copy(heat_next, heat_out, out_sem.at[1]),
    ]
    for copy in outgoing:
        copy.start()

    f0 = split(flux[0])
    f1 = split(flux[1])
    f2 = split(flux[2])
    div[...] = (
        dot(f0[0], along_x[...]) + dot(f0[1], along_x[...])
        + dot(own[0:cells], f1[0]) + dot(own[0:cells], f1[1])
        + dot(own[cells:], f2[0]) + dot(own[cells:], f2[1])
    )
    load_big.wait()
    load_plane.wait()

    def spread(buffer, h):
        lanes = slice(h * part, (h + 1) * part)
        if rows2 % 8 == 0:
            buffer[h] = line[:, lanes].reshape(owners, rows2, part).astype(buffer.dtype)
        else:
            for k in range(owners):
                buffer[h, k] = line[k * rows2 : (k + 1) * rows2, lanes].astype(buffer.dtype)

    def gather(buffer, h):
        if rows2 % 8 == 0:
            return buffer.reshape(owners * rows2, part)
        lanes = slice(h * part, (h + 1) * part)
        for k in range(owners):
            line[k * rows2 : (k + 1) * rows2, lanes] = buffer[k]
        return line[:, lanes]

    def exchange(source, target, send_sem, recv_sem, h, shared=False):
        def begin(oy, oz):
            src = source.at[h, 0] if shared else source.at[h, oy * gz + oz]
            pltpu.make_async_remote_copy(
                src_ref=src, dst_ref=target.at[h, me],
                send_sem=send_sem.at[h], recv_sem=recv_sem.at[h],
                device_id=(oy, oz), device_id_type=mesh_ids,
            ).start()

        to_all(begin)
        target[h, me] = source[h, 0] if shared else source[h, me]

        def done():
            got = target.at[h, 1:owners]
            sent = got if shared else source.at[h, 1:owners]
            pltpu.make_async_copy(got, got, recv_sem.at[h]).wait()
            pltpu.make_async_copy(sent, sent, send_sem.at[h]).wait()

        return done

    def share(source, target, send_sem, recv_sem, h):
        return exchange(source, target, send_sem, recv_sem, h, True)

    def make_factor():
        row = lax.broadcasted_iota(jnp.int32, (2 * m * owners // 2, cells), 0)
        mode = me * m + (row & (m - 1))
        u = (mode - lx // 4).astype(jnp.float32) * (2.0 * np.pi / lx)
        v = u * u
        sine = jnp.zeros_like(u)
        cosine = jnp.zeros_like(u)
        for n in range(9, -1, -1):
            sign = -1.0 if n % 2 else 1.0
            sine = sine * v + sign / float(np.prod(np.arange(1.0, 2 * n + 1)))
            cosine = cosine * v + sign / float(np.prod(np.arange(1.0, 2 * n + 2)))
        cosine = -u * cosine
        kx = (
            1.5 * sine - 0.6 * sine * cosine + sine * (3.0 - 4.0 * sine * sine) * (1.0 / 30.0)
        )
        zero_mode = mode == 0
        kx = jnp.where(zero_mode, 0.0, kx)
        ky, kz = plane[2], plane[3]
        symbol = jnp.zeros_like(kx)
        for c in range(3):
            mixed = metric[c, 0] * kx + metric[c, 1] * ky + metric[c, 2] * kz
            symbol = symbol + mixed * mixed
        at_edge = zero_mode & (plane[4] > 0.5)
        total = float(lx * ey * gy * ez * gz)
        factor[...] = jnp.where(at_edge, 0.0, -1.0 / (jnp.where(at_edge, 1.0, symbol) * total))

    pending = []
    for h in range(parts):
        for copy in f_side[h]:
            copy.wait()
        if h == 0:
            f_top.wait()
        if h == last:
            f_low.wait()
        lo, hi = h * part, (h + 1) * part
        for w in range(2):
            rows = slice(w * ye, (w + 1) * ye)
            halo_f[h, rows] = decode(code_halo_f[h, rows], top_halo_f[h, w])
        e = split(halo_f[h])
        d = split((div[lo:hi] + dot(beside_sum[h], e[0]) + dot(beside_sum[h], e[1])) * sixtieth)
        code, top = encode(dot3((big[0], big[1]), d, 1, 1))
        line[:, lo:hi] = code
        top_line[h, 0] = top
        spread(there, h)
        pending.append(exchange(there, here, a_send, a_recv, h))
        pending.append(share(top_line, tops, u_send, u_recv, h))
    make_factor()

    half = lx // 2
    halved = []
    for h in range(parts):
        pending[2 * h]()
        pending[2 * h + 1]()
        block = gather(decode(here[h], tops[h]), h)
        halved.append(dot3((big[4], big[5]), split(block)))
    out = jnp.concatenate(halved, axis=1)
    re, im = out[:half], out[half:]
    tr, ti = plane[0], plane[1]
    both = jnp.concatenate([re * tr - im * ti, re * ti + im * tr], axis=1)
    out = dot3(split(both), (big[8], big[9]))
    re, im = out[:, :cells] * factor[...], out[:, cells:] * factor[...]
    both = jnp.concatenate([re, im], axis=1)
    out = dot3(split(both), (big[10], big[11]))
    re, im = out[:, :cells], out[:, cells:]
    both = jnp.concatenate([re * tr + im * ti, im * tr - re * ti], axis=0)
    both = split(both)
    pending = []
    for h in range(parts):
        lanes = slice(h * part, (h + 1) * part)
        line[:, lanes] = dot3((big[6], big[7]), [b[:, lanes] for b in both])
        spread(there2, h)
        pending.append(exchange(there2, here2, b_send, b_recv, h))
    side_p, low_p, top_p = borders(press, edge_p, halo_p, p_send, p_recv)
    p_side = []
    for h in range(parts):
        pending[h]()
        lo, hi = h * part, (h + 1) * part
        press[lo:hi] = dot3(split(gather(here2[h], h)), (big[2], big[3]), 0, 0)
        p = split(press[lo:hi], 3)
        edge_p[h] = dot(pick[...], p[0]) + dot(pick[...], p[1]) + dot(pick[...], p[2])
        p_side.append(side_p(h))
        if h == 0:
            p_low = low_p()
    p_top = top_p()
    p = split(press[...], 3)
    grad[0] = dot(own[...], p[0]) + dot(own[...], p[1]) + dot(own[...], p[2])
    grad_x[0] = dot(p[0], along_x[...]) + dot(p[1], along_x[...]) + dot(p[2], along_x[...])
    copy = pltpu.make_async_copy(grad_x.at[0], push_x_out, out_sem.at[2])
    copy.start()
    outgoing.append(copy)
    for h in range(parts):
        for copy in p_side[h]:
            copy.wait()
        if h == 0:
            p_top.wait()
        if h == last:
            p_low.wait()
        lo, hi = h * part, (h + 1) * part
        e = split(halo_p[h], 3)
        more = dot(beside[h], e[0]) + dot(beside[h], e[1]) + dot(beside[h], e[2])
        grad[0, lo:hi] += more[:part]
        grad[0, cells + lo : cells + hi] += more[part:]
        for k, rows in enumerate((slice(lo, hi), slice(cells + lo, cells + hi))):
            copy = pltpu.make_async_copy(
                grad.at[0, rows], push_yz_out.at[rows], out_sem.at[3 + 2 * h + k]
            )
            copy.start()
            outgoing.append(copy)

    for copy in outgoing:
        copy.wait()


def project(metric, prov, push_x, push_y, push_z, heat, motion, heat_next):
    sixtieth = 1.0 / 60.0
    push = [push_x[...] * sixtieth, push_y[...] * sixtieth, push_z[...] * sixtieth]
    for c in range(3):
        motion[c] = prov[c] - (
            metric[c, 0] * push[0] + metric[c, 1] * push[1] + metric[c, 2] * push[2]
        )
    heat_next[...] = heat[...]


def shards(flow_state, metric, deformation):
    gy, gz = lax.axis_size("gy"), lax.axis_size("gz")
    owners = gy * gz
    _, ez, ey, lx = flow_state.shape
    cells = ez * ey
    m = lx // 2 // owners
    own, beside, pick, along_x = stencil_tables(ez, ey, lx)
    cos_x, sin_x, weight = x_tables(lx)
    ahead = by_owner(cos_x, sin_x, owners)
    back = by_owner(cos_x * weight, sin_x * weight, owners)
    twist, kron, block, ky, kz, edge = plane_tables(gy, gz, ey, ez)
    eye = np.eye(m)
    br, bi = np.cos(block), np.sin(block)
    pair = np.stack([np.stack([br, -bi], 1), np.stack([bi, br], 1)], 0)
    across = np.einsum("atsb,mn->atmsbn", pair.transpose(0, 1, 3, 2), eye)
    across = across.reshape(lx, lx)
    wr, wi = np.cos(kron), np.sin(kron)
    within = np.block([[wr, wi], [-wi, wr]])
    big = np.stack(
        halves(ahead) + halves(back) + halves(across) + halves(across.T)
        + halves(within) + halves(within.T)
    )
    plane = np.repeat(
        np.stack([np.cos(twist), np.sin(twist), ky, kz, edge.astype(np.float64)]), m, axis=1
    ).astype(np.float32)
    bf = jnp.bfloat16
    f32 = jnp.float32
    vmem = pl.BlockSpec(memory_space=pltpu.VMEM)
    smem = pl.BlockSpec(memory_space=pltpu.SMEM)
    hbm = pl.BlockSpec(memory_space=pl.ANY)
    zc = ez // parts
    wide = 6 * zc + 4 * ey
    part = zc * ey
    dma = pltpu.SemaphoreType.DMA
    prov, heat, push_x, push_yz = pl.pallas_call(
        lambda *refs: kernel((gy, gz, ez, ey, lx), *refs),
        out_shape=(
            jax.ShapeDtypeStruct((3, cells, lx), f32), jax.ShapeDtypeStruct((cells, lx), f32),
            jax.ShapeDtypeStruct((cells, lx), f32), jax.ShapeDtypeStruct((2 * cells, lx), f32),
        ),
        in_specs=[smem, smem] + [vmem] * 6 + [hbm] * 2,
        out_specs=(hbm,) * 4,
        scratch_shapes=[
            pltpu.VMEM((cells, lx), f32),
            pltpu.VMEM(big.shape, bf),
            pltpu.VMEM(plane.shape, f32),
            pltpu.VMEM((parts, 2, 4, 3 * zc, lx), bf),
            pltpu.VMEM((parts, 4, wide, lx), bf),
            pltpu.VMEM((4, 2 * cells, lx), f32),
            pltpu.VMEM((4, cells, lx), f32),
            pltpu.VMEM((3, cells, lx), f32),
            pltpu.VMEM((3, cells, lx), f32),
            pltpu.VMEM((parts, 6 * zc, lx), f32),
            pltpu.VMEM((parts, wide, lx), f32),
            pltpu.VMEM((cells, lx), f32),
            pltpu.VMEM((parts, 6 * zc, lx), bf),
            pltpu.VMEM((parts, 6 * zc, lx), bf),
            pltpu.VMEM((parts, 1, lx), f32),
            pltpu.VMEM((parts, 2, 1, lx), f32),
            pltpu.VMEM((parts, owners, 1, part), f32),
            pltpu.VMEM((parts, 1, 1, part), f32),
            pltpu.VMEM((parts, 6 * zc, lx), f32),
            pltpu.VMEM((parts, wide, lx), f32),
            pltpu.VMEM((cells, lx), f32),
            pltpu.VMEM((lx, cells), f32),
        ]
        + [pltpu.VMEM((parts, owners, 2 * m, part), bf)] * 2
        + [pltpu.VMEM((parts, owners, 2 * m, part), f32)] * 2
        + [pltpu.VMEM((lx // 2, cells), f32)]
        + [dma((2,)), dma((3 + 2 * parts,))] + [dma((2 * parts,))] * 2 + [dma((parts,))] * 2 + [dma((2 * parts + 2,))] * 6 + [dma((parts,))] * 4,
        compiler_params=pltpu.CompilerParams(
            collective_id=0, has_side_effects=True, vmem_limit_bytes=56 * 2**20
        ),
        cost_estimate=pl.CostEstimate(
            flops=4 * 10**9, bytes_accessed=12 * 2**20, transcendentals=0
        ),
        name="substep",
    )(
        metric, deformation, flow_state.reshape(4, cells, lx),
        jnp.asarray(own, bf), jnp.asarray(beside, bf),
        jnp.asarray(beside[:, :part] + beside[:, part:], bf), jnp.asarray(pick, bf),
        jnp.asarray(along_x, bf), jnp.asarray(big), jnp.asarray(plane),
    )
    steps = 4
    block = cells // steps
    row = pl.BlockSpec((block, lx), lambda i: (i, 0))
    motion, heat_next = pl.pallas_call(
        project,
        grid=(steps,),
        out_shape=(
            jax.ShapeDtypeStruct((3, cells, lx), f32), jax.ShapeDtypeStruct((cells, lx), f32)
        ),
        in_specs=[
            smem, pl.BlockSpec((3, block, lx), lambda i: (0, i, 0)), row, row,
            pl.BlockSpec((block, lx), lambda i: (i + steps, 0)), row,
        ],
        out_specs=(pl.BlockSpec((3, block, lx), lambda i: (0, i, 0)), row),
        compiler_params=pltpu.CompilerParams(vmem_limit_bytes=32 * 2**20),
        name="project",
    )(metric, prov, push_x, push_yz, push_yz, heat)
    return motion.reshape(3, ez, ey, lx), heat_next.reshape(ez, ey, lx)

def solution(mesh):
    placed = (P(None, "gz", "gy", None), P(), P())
    return jax.shard_map(
        shards,
        mesh=mesh,
        in_specs=placed,
        out_specs=(P(None, "gz", "gy", None), P("gz", "gy", None)),
        check_vma=False,
    )
```

```python
import numpy as np

import jax
import jax.numpy as jnp
from jax import lax
from jax.experimental import pallas as pl
from jax.experimental.pallas import tpu as pltpu
from jax.sharding import PartitionSpec as P

substep_width = 0.4
parts = 2
mesh_ids = pl.DeviceIdType.MESH
coefs = {1: 45.0, 2: -9.0, 3: 1.0, -1: -45.0, -2: 9.0, -3: -1.0}


def x_tables(length):
    half = length // 2
    k = np.arange(half)[:, None]
    x = np.arange(length)[None, :]
    angle = 2.0 * np.pi * ((k * x) % length) / length
    c, s = np.cos(angle), -np.sin(angle)
    s[0] = np.where(np.arange(length) % 2 == 0, 1.0, -1.0)
    weight = np.where(np.arange(half) == 0, 1.0, 2.0)[:, None]
    return c, s, weight


def by_owner(re, im, owners):
    half, length = re.shape
    m = half // owners
    return np.concatenate(
        [re.reshape(owners, m, length), im.reshape(owners, m, length)], axis=1
    ).reshape(2 * half, length)


def wave(m, length):
    a = 2.0 * np.pi * m / length
    value = 1.5 * np.sin(a) - 0.3 * np.sin(2 * a) + np.sin(3 * a) / 30.0
    return np.where((2 * m) % length == 0, 0.0, value)


def plane_tables(gy, gz, ey, ez):
    ly, lz = gy * ey, gz * ez
    b = np.repeat(np.arange(ez), ey)
    e = np.tile(np.arange(ey), ez)
    s = np.repeat(np.arange(gy), gz)[:, None]
    q = np.tile(np.arange(gz), gy)[:, None]
    twist = -2.0 * np.pi * (b * q / lz + e * s / ly)
    kron = -2.0 * np.pi * (np.outer(b, b) / ez + np.outer(e, e) / ey)
    my = gy * e[None, :] + s
    mz = gz * b[None, :] + q
    block = -2.0 * np.pi * (
        np.outer(s, s) / gy + np.outer(q, q) / gz
    )
    edge = ((2 * my) % ly == 0) & ((2 * mz) % lz == 0)
    return twist, kron, block, wave(my, ly), wave(mz, lz), edge


def stencil_tables(ez, ey, lx):
    cells, zc = ez * ey, ez // parts
    part = zc * ey
    own = np.zeros((2 * cells, cells))
    beside = np.zeros((parts, 2 * part, 6 * zc + 4 * ey))
    pick = np.zeros((6 * zc, part))
    for z in range(ez):
        h, zh = z // zc, z % zc
        for y in range(ey):
            r, rh = z * ey + y, zh * ey + y
            for o, w in coefs.items():
                t = y + o
                if 0 <= t < ey:
                    own[r, z * ey + t] += w
                elif t < 0:
                    beside[h, rh, (t + 3) * zc + zh] += w
                else:
                    beside[h, rh, (3 + t - ey) * zc + zh] += w
                t = z + o
                if 0 <= t < ez:
                    own[cells + r, t * ey + y] += w
                elif t < 0:
                    beside[h, part + rh, 6 * zc + (t + 4) * ey + y] += w
                else:
                    beside[h, part + rh, 6 * zc + (t - ez) * ey + y] += w
        for j in range(3):
            pick[j * zc + zh, zh * ey + ey - 3 + j] = 1.0
            pick[(3 + j) * zc + zh, zh * ey + j] = 1.0
    along_x = np.zeros((lx, lx))
    for o, w in coefs.items():
        x = np.arange(lx)
        along_x[(x + o) % lx, x] += w
    return own, beside, pick, along_x


def halves(a):
    a = np.asarray(a, np.float32)
    top = a.astype(jnp.bfloat16)
    return [top, (a - top.astype(np.float32)).astype(jnp.bfloat16)]


def split(x, pieces=2):
    out = []
    for _ in range(pieces):
        top = x.astype(jnp.bfloat16)
        out.append(top)
        x = x - top.astype(jnp.float32)
    return out


code_top = 2.0**7.5


def encode(x):
    top = jnp.maximum(jnp.max(jnp.abs(x), axis=0, keepdims=True), 1e-30)
    t = x * (code_top / top)
    for _ in range(4):
        t = t * t
    return jnp.where(x < 0.0, -t, t), top


def decode(code, top):
    code = code.astype(jnp.float32)
    size = jnp.abs(code)
    root = jnp.exp(jnp.log(jnp.maximum(size, 1e-37)) * (1.0 / 16.0)) * (top * (1.0 / code_top))
    root = jnp.where(size < 1e-37, 0.0, root)
    return jnp.where(code < 0.0, -root, root)


def dot(a, b, ca=1, cb=0):
    return lax.dot_general(a, b, (((ca,), (cb,)), ((), ())), preferred_element_type=jnp.float32)


def dot3(a, b, ca=1, cb=0):
    return dot(a[0], b[0], ca, cb) + dot(a[0], b[1], ca, cb) + dot(a[1], b[0], ca, cb)


def kernel(
    sizes, metric, deform, state, own, beside, beside_sum, pick, along_x, big_hbm, plane_hbm,
    prov_out, heat_out, push_x_out, push_yz_out,
    heat_next, big, plane, edge_state, halo_state, grad, grad_x, prov, flux, edge_f, halo_f, div, code_f, code_halo_f, top_f, top_halo_f, tops, top_line,
    edge_p, halo_p, press, line, there, here, there2, here2, factor,
    load_sem, out_sem, t_send, t_recv, u_send, u_recv, s_send, s_recv, f_send, f_recv, p_send, p_recv, a_send, a_recv, b_send, b_recv,
):
    gy, gz, ez, ey, lx = sizes
    owners = gy * gz
    cells = ez * ey
    rows2 = lx // owners
    m = rows2 // 2
    zc = ez // parts
    part = zc * ey
    ye, ze = 3 * zc, 4 * ey
    last = parts - 1
    iy, iz = lax.axis_index("gy"), lax.axis_index("gz")
    me = iy * gz + iz
    up_y = (lax.rem(iy + 1, gy), iz)
    down_y = (lax.rem(iy + gy - 1, gy), iz)
    up_z = (iy, lax.rem(iz + 1, gz))
    down_z = (iy, lax.rem(iz + gz - 1, gz))

    load_big = pltpu.make_async_copy(big_hbm, big, load_sem.at[0])
    load_plane = pltpu.make_async_copy(plane_hbm, plane, load_sem.at[1])
    load_big.start()
    load_plane.start()

    def to_all(begin):
        for dz in range(1, gz):
            begin(iy, lax.rem(iz + dz, gz))

        def ring(dy, carry):
            oy = lax.rem(iy + dy, gy)
            for dz in range(gz):
                begin(oy, lax.rem(iz + dz, gz))
            return carry

        lax.fori_loop(1, gy, ring, 0)

    barrier = pltpu.get_barrier_semaphore()

    def greet(oy, oz):
        pl.semaphore_signal(barrier, inc=1, device_id=(oy, oz), device_id_type=mesh_ids)

    to_all(greet)

    for h in range(parts):
        for c in range(4):
            picked = dot(pick[...], state[c, h * part : (h + 1) * part]).astype(jnp.bfloat16)
            edge_state[h, 0, c] = picked[:ye]
            edge_state[h, 1, c] = picked[ye:]
    pl.semaphore_wait(barrier, owners - 1)

    def send(src, dst, send_sem, recv_sem, to):
        copy = pltpu.make_async_remote_copy(
            src_ref=src, dst_ref=dst, send_sem=send_sem, recv_sem=recv_sem,
            device_id=to, device_id_type=mesh_ids,
        )
        copy.start()
        return copy

    side_y = [
        [
            send(
                edge_state.at[h, w], halo_state.at[h, :, w * ye : (w + 1) * ye],
                s_send.at[2 * h + w], s_recv.at[2 * h + w], (up_y, down_y)[w],
            )
            for w in range(2)
        ]
        for h in range(parts)
    ]
    side_z = [
        send(
            state.at[:, cells - ze : cells], halo_state.at[0, :, 2 * ye : 2 * ye + ze],
            s_send.at[2 * parts], s_recv.at[2 * parts], up_z,
        ),
        send(
            state.at[:, 0:ze], halo_state.at[last, :, 2 * ye : 2 * ye + ze],
            s_send.at[2 * parts + 1], s_recv.at[2 * parts + 1], down_z,
        ),
    ]
    for c in range(4):
        grad[c] = dot(own[...], state[c])
        grad_x[c] = dot(state[c], along_x[...])

    def make_factor():
        row = lax.broadcasted_iota(jnp.int32, (2 * m * owners // 2, cells), 0)
        mode = me * m + (row & (m - 1))
        u = (mode - lx // 4).astype(jnp.float32) * (2.0 * np.pi / lx)
        v = u * u
        sine = jnp.zeros_like(u)
        cosine = jnp.zeros_like(u)
        for n in range(9, -1, -1):
            sign = -1.0 if n % 2 else 1.0
            sine = sine * v + sign / float(np.prod(np.arange(1.0, 2 * n + 1)))
            cosine = cosine * v + sign / float(np.prod(np.arange(1.0, 2 * n + 2)))
        cosine = -u * cosine
        kx = (
            1.5 * sine - 0.6 * sine * cosine + sine * (3.0 - 4.0 * sine * sine) * (1.0 / 30.0)
        )
        zero_mode = mode == 0
        kx = jnp.where(zero_mode, 0.0, kx)
        ky, kz = plane[2], plane[3]
        symbol = jnp.zeros_like(kx)
        for c in range(3):
            mixed = metric[c, 0] * kx + metric[c, 1] * ky + metric[c, 2] * kz
            symbol = symbol + mixed * mixed
        at_edge = zero_mode & (plane[4] > 0.5)
        total = float(lx * ey * gy * ez * gz)
        factor[...] = jnp.where(at_edge, 0.0, -1.0 / (jnp.where(at_edge, 1.0, symbol) * total))

    load_plane.wait()
    make_factor()
    load_big.wait()

    def borders(field, edges, halo, sends, recvs):
        def side(h, edges=edges, halo=halo):
            return [
                send(
                    edges.at[h, w * ye : (w + 1) * ye], halo.at[h, w * ye : (w + 1) * ye],
                    sends.at[2 * h + w], recvs.at[2 * h + w], (up_y, down_y)[w],
                )
                for w in range(2)
            ]

        def low():
            return send(
                field.at[0:ze], halo.at[last, 2 * ye : 2 * ye + ze],
                sends.at[2 * parts + 1], recvs.at[2 * parts + 1], down_z,
            )

        def top():
            return send(
                field.at[cells - ze : cells], halo.at[0, 2 * ye : 2 * ye + ze],
                sends.at[2 * parts], recvs.at[2 * parts], up_z,
            )

        return side, low, top

    sixtieth = 1.0 / 60.0

    def advance(i, carry):
        rows = pl.ds(pl.multiple_of(i * 16, 16), 16)
        rows_z = pl.ds(pl.multiple_of(cells + i * 16, 16), 16)
        f = [state[c, rows, :].astype(jnp.float32) for c in range(4)]
        contra = [
            (metric[0, j] * f[0] + metric[1, j] * f[1] + metric[2, j] * f[2]) * sixtieth
            for j in range(3)
        ]
        carried = [
            contra[0] * grad_x[c, rows, :]
            + contra[1] * grad[c, rows, :]
            + contra[2] * grad[c, rows_z, :]
            for c in range(4)
        ]
        new = []
        for c in range(3):
            change = -carried[c] - (
                deform[c, 0] * f[0] + deform[c, 1] * f[1] + deform[c, 2] * f[2]
            )
            if c == 2:
                change = change + f[3]
            new.append(f[c] + substep_width * change)
            prov[c, rows, :] = new[c]
        heat_next[rows, :] = f[3] + substep_width * (-carried[3] - f[2])
        for j in range(3):
            flux[j, rows, :] = metric[0, j] * new[0] + metric[1, j] * new[1] + metric[2, j] * new[2]
        return carry

    side_f, low_f, high_f = borders(flux.at[2], edge_f, halo_f, f_send, f_recv)
    f_side = []
    for h in range(parts):
        for copy in side_y[h]:
            copy.wait()
        if h == 0:
            for copy in side_z:
                copy.wait()
        lo, hi = h * part, (h + 1) * part
        for c in range(4):
            more = dot(beside[h], halo_state[h, c])
            grad[c, lo:hi] += more[:part]
            grad[c, cells + lo : cells + hi] += more[part:]
        lax.fori_loop(lo // 16, hi // 16, advance, 0)
        f1 = split(flux[1, lo:hi])
        code, top = encode(dot(pick[...], f1[0]) + dot(pick[...], f1[1]))
        code_f[h] = code.astype(jnp.bfloat16)
        top_f[h] = top
        f_side.append(
            side_f(h, code_f, code_halo_f)
            + [
                send(
                    top_f.at[h], top_halo_f.at[h, w], t_send.at[2 * h + w], t_recv.at[2 * h + w],
                    (up_y, down_y)[w],
                )
                for w in range(2)
            ]
        )
        if h == 0:
            f_low = low_f()
    f_top = high_f()
    outgoing = [
        pltpu.make_async_copy(prov, prov_out, out_sem.at[0]),
        pltpu.make_async_copy(heat_next, heat_out, out_sem.at[1]),
    ]
    for copy in outgoing:
        copy.start()

    f0 = split(flux[0])
    f1 = split(flux[1])
    f2 = split(flux[2])
    div[...] = (
        dot(f0[0], along_x[...]) + dot(f0[1], along_x[...])
        + dot(own[0:cells], f1[0]) + dot(own[0:cells], f1[1])
        + dot(own[cells:], f2[0]) + dot(own[cells:], f2[1])
    )
    def spread(buffer, h):
        lanes = slice(h * part, (h + 1) * part)
        if rows2 % 8 == 0:
            buffer[h] = line[:, lanes].reshape(owners, rows2, part).astype(buffer.dtype)
        else:
            for k in range(owners):
                buffer[h, k] = line[k * rows2 : (k + 1) * rows2, lanes].astype(buffer.dtype)

    def gather(buffer, h):
        if rows2 % 8 == 0:
            return buffer.reshape(owners * rows2, part)
        lanes = slice(h * part, (h + 1) * part)
        for k in range(owners):
            line[k * rows2 : (k + 1) * rows2, lanes] = buffer[k]
        return line[:, lanes]

    def exchange(source, target, send_sem, recv_sem, h, shared=False):
        def begin(oy, oz):
            src = source.at[h, 0] if shared else source.at[h, oy * gz + oz]
            pltpu.make_async_remote_copy(
                src_ref=src, dst_ref=target.at[h, me],
                send_sem=send_sem.at[h], recv_sem=recv_sem.at[h],
                device_id=(oy, oz), device_id_type=mesh_ids,
            ).start()

        to_all(begin)
        target[h, me] = source[h, 0] if shared else source[h, me]

        def done():
            got = target.at[h, 1:owners]
            sent = got if shared else source.at[h, 1:owners]
            pltpu.make_async_copy(got, got, recv_sem.at[h]).wait()
            pltpu.make_async_copy(sent, sent, send_sem.at[h]).wait()

        return done

    def share(source, target, send_sem, recv_sem, h):
        return exchange(source, target, send_sem, recv_sem, h, True)

    pending = []
    for h in range(parts):
        for copy in f_side[h]:
            copy.wait()
        if h == 0:
            f_top.wait()
        if h == last:
            f_low.wait()
        lo, hi = h * part, (h + 1) * part
        for w in range(2):
            rows = slice(w * ye, (w + 1) * ye)
            halo_f[h, rows] = decode(code_halo_f[h, rows], top_halo_f[h, w])
        e = split(halo_f[h])
        d = split((div[lo:hi] + dot(beside_sum[h], e[0]) + dot(beside_sum[h], e[1])) * sixtieth)
        code, top = encode(dot3((big[0], big[1]), d, 1, 1))
        line[:, lo:hi] = code
        top_line[h, 0] = top
        spread(there, h)
        pending.append(exchange(there, here, a_send, a_recv, h))
        pending.append(share(top_line, tops, u_send, u_recv, h))

    half = lx // 2
    halved = []
    for h in range(parts):
        pending[2 * h]()
        pending[2 * h + 1]()
        block = gather(decode(here[h], tops[h]), h)
        halved.append(dot3((big[4], big[5]), split(block)))
    out = jnp.concatenate(halved, axis=1)
    re, im = out[:half], out[half:]
    tr, ti = plane[0], plane[1]
    both = jnp.concatenate([re * tr - im * ti, re * ti + im * tr], axis=1)
    out = dot3(split(both), (big[8], big[9]))
    re, im = out[:, :cells] * factor[...], out[:, cells:] * factor[...]
    both = jnp.concatenate([re, im], axis=1)
    out = dot3(split(both), (big[10], big[11]))
    re, im = out[:, :cells], out[:, cells:]
    both = jnp.concatenate([re * tr + im * ti, im * tr - re * ti], axis=0)
    both = split(both)
    pending = []
    for h in range(parts):
        lanes = slice(h * part, (h + 1) * part)
        line[:, lanes] = dot3((big[6], big[7]), [b[:, lanes] for b in both])
        spread(there2, h)
        pending.append(exchange(there2, here2, b_send, b_recv, h))
    side_p, low_p, top_p = borders(press, edge_p, halo_p, p_send, p_recv)
    p_side = []
    for h in range(parts):
        pending[h]()
        lo, hi = h * part, (h + 1) * part
        press[lo:hi] = dot3(split(gather(here2[h], h)), (big[2], big[3]), 0, 0)
        p = split(press[lo:hi], 3)
        edge_p[h] = dot(pick[...], p[0]) + dot(pick[...], p[1]) + dot(pick[...], p[2])
        p_side.append(side_p(h))
        if h == 0:
            p_low = low_p()
    p_top = top_p()
    p = split(press[...], 3)
    grad[0] = dot(own[...], p[0]) + dot(own[...], p[1]) + dot(own[...], p[2])
    grad_x[0] = dot(p[0], along_x[...]) + dot(p[1], along_x[...]) + dot(p[2], along_x[...])
    copy = pltpu.make_async_copy(grad_x.at[0], push_x_out, out_sem.at[2])
    copy.start()
    outgoing.append(copy)
    for h in range(parts):
        for copy in p_side[h]:
            copy.wait()
        if h == 0:
            p_top.wait()
        if h == last:
            p_low.wait()
        lo, hi = h * part, (h + 1) * part
        e = split(halo_p[h], 3)
        more = dot(beside[h], e[0]) + dot(beside[h], e[1]) + dot(beside[h], e[2])
        grad[0, lo:hi] += more[:part]
        grad[0, cells + lo : cells + hi] += more[part:]
        for k, rows in enumerate((slice(lo, hi), slice(cells + lo, cells + hi))):
            copy = pltpu.make_async_copy(
                grad.at[0, rows], push_yz_out.at[rows], out_sem.at[3 + 2 * h + k]
            )
            copy.start()
            outgoing.append(copy)

    for copy in outgoing:
        copy.wait()


def project(metric, prov, push_x, push_y, push_z, heat, motion, heat_next):
    sixtieth = 1.0 / 60.0
    push = [push_x[...] * sixtieth, push_y[...] * sixtieth, push_z[...] * sixtieth]
    for c in range(3):
        motion[c] = prov[c] - (
            metric[c, 0] * push[0] + metric[c, 1] * push[1] + metric[c, 2] * push[2]
        )
    heat_next[...] = heat[...]


def shards(flow_state, metric, deformation):
    gy, gz = lax.axis_size("gy"), lax.axis_size("gz")
    owners = gy * gz
    _, ez, ey, lx = flow_state.shape
    cells = ez * ey
    m = lx // 2 // owners
    own, beside, pick, along_x = stencil_tables(ez, ey, lx)
    cos_x, sin_x, weight = x_tables(lx)
    ahead = by_owner(cos_x, sin_x, owners)
    back = by_owner(cos_x * weight, sin_x * weight, owners)
    twist, kron, block, ky, kz, edge = plane_tables(gy, gz, ey, ez)
    eye = np.eye(m)
    br, bi = np.cos(block), np.sin(block)
    pair = np.stack([np.stack([br, -bi], 1), np.stack([bi, br], 1)], 0)
    across = np.einsum("atsb,mn->atmsbn", pair.transpose(0, 1, 3, 2), eye)
    across = across.reshape(lx, lx)
    wr, wi = np.cos(kron), np.sin(kron)
    within = np.block([[wr, wi], [-wi, wr]])
    big = np.stack(
        halves(ahead) + halves(back) + halves(across) + halves(across.T)
        + halves(within) + halves(within.T)
    )
    plane = np.repeat(
        np.stack([np.cos(twist), np.sin(twist), ky, kz, edge.astype(np.float64)]), m, axis=1
    ).astype(np.float32)
    bf = jnp.bfloat16
    f32 = jnp.float32
    vmem = pl.BlockSpec(memory_space=pltpu.VMEM)
    smem = pl.BlockSpec(memory_space=pltpu.SMEM)
    hbm = pl.BlockSpec(memory_space=pl.ANY)
    zc = ez // parts
    wide = 6 * zc + 4 * ey
    part = zc * ey
    dma = pltpu.SemaphoreType.DMA
    prov, heat, push_x, push_yz = pl.pallas_call(
        lambda *refs: kernel((gy, gz, ez, ey, lx), *refs),
        out_shape=(
            jax.ShapeDtypeStruct((3, cells, lx), f32), jax.ShapeDtypeStruct((cells, lx), f32),
            jax.ShapeDtypeStruct((cells, lx), f32), jax.ShapeDtypeStruct((2 * cells, lx), f32),
        ),
        in_specs=[smem, smem] + [vmem] * 6 + [hbm] * 2,
        out_specs=(hbm,) * 4,
        scratch_shapes=[
            pltpu.VMEM((cells, lx), f32),
            pltpu.VMEM(big.shape, bf),
            pltpu.VMEM(plane.shape, f32),
            pltpu.VMEM((parts, 2, 4, 3 * zc, lx), bf),
            pltpu.VMEM((parts, 4, wide, lx), bf),
            pltpu.VMEM((4, 2 * cells, lx), f32),
            pltpu.VMEM((4, cells, lx), f32),
            pltpu.VMEM((3, cells, lx), f32),
            pltpu.VMEM((3, cells, lx), f32),
            pltpu.VMEM((parts, 6 * zc, lx), f32),
            pltpu.VMEM((parts, wide, lx), f32),
            pltpu.VMEM((cells, lx), f32),
            pltpu.VMEM((parts, 6 * zc, lx), bf),
            pltpu.VMEM((parts, 6 * zc, lx), bf),
            pltpu.VMEM((parts, 1, lx), f32),
            pltpu.VMEM((parts, 2, 1, lx), f32),
            pltpu.VMEM((parts, owners, 1, part), f32),
            pltpu.VMEM((parts, 1, 1, part), f32),
            pltpu.VMEM((parts, 6 * zc, lx), f32),
            pltpu.VMEM((parts, wide, lx), f32),
            pltpu.VMEM((cells, lx), f32),
            pltpu.VMEM((lx, cells), f32),
        ]
        + [pltpu.VMEM((parts, owners, 2 * m, part), bf)] * 2
        + [pltpu.VMEM((parts, owners, 2 * m, part), f32)] * 2
        + [pltpu.VMEM((lx // 2, cells), f32)]
        + [dma((2,)), dma((3 + 2 * parts,))] + [dma((2 * parts,))] * 2 + [dma((parts,))] * 2 + [dma((2 * parts + 2,))] * 6 + [dma((parts,))] * 4,
        compiler_params=pltpu.CompilerParams(
            collective_id=0, has_side_effects=True, vmem_limit_bytes=56 * 2**20
        ),
        cost_estimate=pl.CostEstimate(
            flops=4 * 10**9, bytes_accessed=12 * 2**20, transcendentals=0
        ),
        name="substep",
    )(
        metric, deformation, flow_state.reshape(4, cells, lx),
        jnp.asarray(own, bf), jnp.asarray(beside, bf),
        jnp.asarray(beside[:, :part] + beside[:, part:], bf), jnp.asarray(pick, bf),
        jnp.asarray(along_x, bf), jnp.asarray(big), jnp.asarray(plane),
    )
    steps = 4
    block = cells // steps
    row = pl.BlockSpec((block, lx), lambda i: (i, 0))
    motion, heat_next = pl.pallas_call(
        project,
        grid=(steps,),
        out_shape=(
            jax.ShapeDtypeStruct((3, cells, lx), f32), jax.ShapeDtypeStruct((cells, lx), f32)
        ),
        in_specs=[
            smem, pl.BlockSpec((3, block, lx), lambda i: (0, i, 0)), row, row,
            pl.BlockSpec((block, lx), lambda i: (i + steps, 0)), row,
        ],
        out_specs=(pl.BlockSpec((3, block, lx), lambda i: (0, i, 0)), row),
        compiler_params=pltpu.CompilerParams(vmem_limit_bytes=60 * 2**20),
        name="project",
    )(metric, prov, push_x, push_yz, push_yz, heat)
    return motion.reshape(3, ez, ey, lx), heat_next.reshape(ez, ey, lx)

def solution(mesh):
    placed = (P(None, "gz", "gy", None), P(), P())
    return jax.shard_map(
        shards,
        mesh=mesh,
        in_specs=placed,
        out_specs=(P(None, "gz", "gy", None), P("gz", "gy", None)),
        check_vma=False,
    )
```

```python
import numpy as np

import jax
import jax.numpy as jnp
from jax import lax
from jax.experimental import pallas as pl
from jax.experimental.pallas import tpu as pltpu
from jax.sharding import PartitionSpec as P

substep_width = 0.4
parts = 2
mesh_ids = pl.DeviceIdType.MESH
coefs = {1: 45.0, 2: -9.0, 3: 1.0, -1: -45.0, -2: 9.0, -3: -1.0}


def x_tables(length):
    half = length // 2
    k = np.arange(half)[:, None]
    x = np.arange(length)[None, :]
    angle = 2.0 * np.pi * ((k * x) % length) / length
    c, s = np.cos(angle), -np.sin(angle)
    s[0] = np.where(np.arange(length) % 2 == 0, 1.0, -1.0)
    weight = np.where(np.arange(half) == 0, 1.0, 2.0)[:, None]
    return c, s, weight


def by_owner(re, im, owners):
    half, length = re.shape
    m = half // owners
    return np.concatenate(
        [re.reshape(owners, m, length), im.reshape(owners, m, length)], axis=1
    ).reshape(2 * half, length)


def wave(m, length):
    a = 2.0 * np.pi * m / length
    value = 1.5 * np.sin(a) - 0.3 * np.sin(2 * a) + np.sin(3 * a) / 30.0
    return np.where((2 * m) % length == 0, 0.0, value)


def plane_tables(gy, gz, ey, ez):
    ly, lz = gy * ey, gz * ez
    b = np.repeat(np.arange(ez), ey)
    e = np.tile(np.arange(ey), ez)
    s = np.repeat(np.arange(gy), gz)[:, None]
    q = np.tile(np.arange(gz), gy)[:, None]
    twist = -2.0 * np.pi * (b * q / lz + e * s / ly)
    kron = -2.0 * np.pi * (np.outer(b, b) / ez + np.outer(e, e) / ey)
    my = gy * e[None, :] + s
    mz = gz * b[None, :] + q
    block = -2.0 * np.pi * (
        np.outer(s, s) / gy + np.outer(q, q) / gz
    )
    edge = ((2 * my) % ly == 0) & ((2 * mz) % lz == 0)
    return twist, kron, block, wave(my, ly), wave(mz, lz), edge


def stencil_tables(ez, ey, lx):
    cells, zc = ez * ey, ez // parts
    part = zc * ey
    own = np.zeros((2 * cells, cells))
    beside = np.zeros((parts, 2 * part, 6 * zc + 4 * ey))
    pick = np.zeros((6 * zc, part))
    for z in range(ez):
        h, zh = z // zc, z % zc
        for y in range(ey):
            r, rh = z * ey + y, zh * ey + y
            for o, w in coefs.items():
                t = y + o
                if 0 <= t < ey:
                    own[r, z * ey + t] += w
                elif t < 0:
                    beside[h, rh, (t + 3) * zc + zh] += w
                else:
                    beside[h, rh, (3 + t - ey) * zc + zh] += w
                t = z + o
                if 0 <= t < ez:
                    own[cells + r, t * ey + y] += w
                elif t < 0:
                    beside[h, part + rh, 6 * zc + (t + 4) * ey + y] += w
                else:
                    beside[h, part + rh, 6 * zc + (t - ez) * ey + y] += w
        for j in range(3):
            pick[j * zc + zh, zh * ey + ey - 3 + j] = 1.0
            pick[(3 + j) * zc + zh, zh * ey + j] = 1.0
    along_x = np.zeros((lx, lx))
    for o, w in coefs.items():
        x = np.arange(lx)
        along_x[(x + o) % lx, x] += w
    return own, beside, pick, along_x


def halves(a):
    a = np.asarray(a, np.float32)
    top = a.astype(jnp.bfloat16)
    return [top, (a - top.astype(np.float32)).astype(jnp.bfloat16)]


def split(x, pieces=2):
    out = []
    for _ in range(pieces):
        top = x.astype(jnp.bfloat16)
        out.append(top)
        x = x - top.astype(jnp.float32)
    return out


code_top = 2.0**7.5


def encode(x):
    top = jnp.maximum(jnp.max(jnp.abs(x), axis=0, keepdims=True), 1e-30)
    t = x * (code_top / top)
    for _ in range(4):
        t = t * t
    return jnp.where(x < 0.0, -t, t), top


def decode(code, top):
    code = code.astype(jnp.float32)
    size = jnp.abs(code)
    root = jnp.exp(jnp.log(jnp.maximum(size, 1e-37)) * (1.0 / 16.0)) * (top * (1.0 / code_top))
    root = jnp.where(size < 1e-37, 0.0, root)
    return jnp.where(code < 0.0, -root, root)


def dot(a, b, ca=1, cb=0):
    return lax.dot_general(a, b, (((ca,), (cb,)), ((), ())), preferred_element_type=jnp.float32)


def dot3(a, b, ca=1, cb=0):
    return dot(a[0], b[0], ca, cb) + dot(a[0], b[1], ca, cb) + dot(a[1], b[0], ca, cb)


def kernel(
    sizes, metric, deform, state_hbm, own_hbm, beside_hbm, beside_sum_hbm, pick, along_x_hbm,
    big_hbm, plane_hbm, motion_out, heat_out,
    state, own, beside, beside_sum, along_x, heat_next, big, plane, edge_state, halo_state, grad, grad_x, prov, flux, edge_f, halo_f, div, code_f, code_halo_f, top_f, top_halo_f, tops, top_line,
    edge_p, halo_p, press, line, there, here, there2, here2, factor,
    load_sem, out_sem, t_send, t_recv, u_send, u_recv, s_send, s_recv, f_send, f_recv, p_send, p_recv, a_send, a_recv, b_send, b_recv,
):
    gy, gz, ez, ey, lx = sizes
    owners = gy * gz
    cells = ez * ey
    rows2 = lx // owners
    m = rows2 // 2
    zc = ez // parts
    part = zc * ey
    ye, ze = 3 * zc, 4 * ey
    last = parts - 1
    iy, iz = lax.axis_index("gy"), lax.axis_index("gz")
    me = iy * gz + iz
    up_y = (lax.rem(iy + 1, gy), iz)
    down_y = (lax.rem(iy + gy - 1, gy), iz)
    up_z = (iy, lax.rem(iz + 1, gz))
    down_z = (iy, lax.rem(iz + gz - 1, gz))

    load_state = pltpu.make_async_copy(state_hbm, state, load_sem.at[2])
    load_state.start()
    loads = [
        pltpu.make_async_copy(source, target, load_sem.at[3 + k])
        for k, (source, target) in enumerate(
            ((own_hbm, own), (along_x_hbm, along_x), (beside_hbm, beside), (beside_sum_hbm, beside_sum))
        )
    ]
    load_big = pltpu.make_async_copy(big_hbm, big, load_sem.at[0])
    load_plane = pltpu.make_async_copy(plane_hbm, plane, load_sem.at[1])
    def to_all(begin):
        for dz in range(1, gz):
            begin(iy, lax.rem(iz + dz, gz))

        def ring(dy, carry):
            oy = lax.rem(iy + dy, gy)
            for dz in range(gz):
                begin(oy, lax.rem(iz + dz, gz))
            return carry

        lax.fori_loop(1, gy, ring, 0)

    barrier = pltpu.get_barrier_semaphore()

    def greet(oy, oz):
        pl.semaphore_signal(barrier, inc=1, device_id=(oy, oz), device_id_type=mesh_ids)

    to_all(greet)
    for copy in loads:
        copy.start()
    load_plane.start()
    load_big.start()
    load_state.wait()

    for h in range(parts):
        for c in range(4):
            picked = dot(pick[...], state[c, h * part : (h + 1) * part]).astype(jnp.bfloat16)
            edge_state[h, 0, c] = picked[:ye]
            edge_state[h, 1, c] = picked[ye:]
    pl.semaphore_wait(barrier, owners - 1)

    def send(src, dst, send_sem, recv_sem, to):
        copy = pltpu.make_async_remote_copy(
            src_ref=src, dst_ref=dst, send_sem=send_sem, recv_sem=recv_sem,
            device_id=to, device_id_type=mesh_ids,
        )
        copy.start()
        return copy

    side_y = [
        [
            send(
                edge_state.at[h, w], halo_state.at[h, :, w * ye : (w + 1) * ye],
                s_send.at[2 * h + w], s_recv.at[2 * h + w], (up_y, down_y)[w],
            )
            for w in range(2)
        ]
        for h in range(parts)
    ]
    side_z = [
        send(
            state.at[:, cells - ze : cells], halo_state.at[0, :, 2 * ye : 2 * ye + ze],
            s_send.at[2 * parts], s_recv.at[2 * parts], up_z,
        ),
        send(
            state.at[:, 0:ze], halo_state.at[last, :, 2 * ye : 2 * ye + ze],
            s_send.at[2 * parts + 1], s_recv.at[2 * parts + 1], down_z,
        ),
    ]
    for copy in loads:
        copy.wait()
    for c in range(4):
        grad[c] = dot(own[...], state[c])
        grad_x[c] = dot(state[c], along_x[...])

    def make_factor():
        row = lax.broadcasted_iota(jnp.int32, (2 * m * owners // 2, cells), 0)
        mode = me * m + (row & (m - 1))
        u = (mode - lx // 4).astype(jnp.float32) * (2.0 * np.pi / lx)
        v = u * u
        sine = jnp.zeros_like(u)
        cosine = jnp.zeros_like(u)
        for n in range(9, -1, -1):
            sign = -1.0 if n % 2 else 1.0
            sine = sine * v + sign / float(np.prod(np.arange(1.0, 2 * n + 1)))
            cosine = cosine * v + sign / float(np.prod(np.arange(1.0, 2 * n + 2)))
        cosine = -u * cosine
        kx = (
            1.5 * sine - 0.6 * sine * cosine + sine * (3.0 - 4.0 * sine * sine) * (1.0 / 30.0)
        )
        zero_mode = mode == 0
        kx = jnp.where(zero_mode, 0.0, kx)
        ky, kz = plane[2], plane[3]
        symbol = jnp.zeros_like(kx)
        for c in range(3):
            mixed = metric[c, 0] * kx + metric[c, 1] * ky + metric[c, 2] * kz
            symbol = symbol + mixed * mixed
        at_edge = zero_mode & (plane[4] > 0.5)
        total = float(lx * ey * gy * ez * gz)
        factor[...] = jnp.where(at_edge, 0.0, -1.0 / (jnp.where(at_edge, 1.0, symbol) * total))

    load_plane.wait()
    make_factor()
    load_big.wait()

    def borders(field, edges, halo, sends, recvs):
        def side(h, edges=edges, halo=halo):
            return [
                send(
                    edges.at[h, w * ye : (w + 1) * ye], halo.at[h, w * ye : (w + 1) * ye],
                    sends.at[2 * h + w], recvs.at[2 * h + w], (up_y, down_y)[w],
                )
                for w in range(2)
            ]

        def low():
            return send(
                field.at[0:ze], halo.at[last, 2 * ye : 2 * ye + ze],
                sends.at[2 * parts + 1], recvs.at[2 * parts + 1], down_z,
            )

        def top():
            return send(
                field.at[cells - ze : cells], halo.at[0, 2 * ye : 2 * ye + ze],
                sends.at[2 * parts], recvs.at[2 * parts], up_z,
            )

        return side, low, top

    sixtieth = 1.0 / 60.0

    def advance(i, carry):
        rows = pl.ds(pl.multiple_of(i * 16, 16), 16)
        rows_z = pl.ds(pl.multiple_of(cells + i * 16, 16), 16)
        f = [state[c, rows, :].astype(jnp.float32) for c in range(4)]
        contra = [
            (metric[0, j] * f[0] + metric[1, j] * f[1] + metric[2, j] * f[2]) * sixtieth
            for j in range(3)
        ]
        carried = [
            contra[0] * grad_x[c, rows, :]
            + contra[1] * grad[c, rows, :]
            + contra[2] * grad[c, rows_z, :]
            for c in range(4)
        ]
        new = []
        for c in range(3):
            change = -carried[c] - (
                deform[c, 0] * f[0] + deform[c, 1] * f[1] + deform[c, 2] * f[2]
            )
            if c == 2:
                change = change + f[3]
            new.append(f[c] + substep_width * change)
            prov[c, rows, :] = new[c]
        heat_next[rows, :] = f[3] + substep_width * (-carried[3] - f[2])
        for j in range(3):
            flux[j, rows, :] = metric[0, j] * new[0] + metric[1, j] * new[1] + metric[2, j] * new[2]
        return carry

    side_f, low_f, high_f = borders(flux.at[2], edge_f, halo_f, f_send, f_recv)
    f_side = []
    for h in range(parts):
        for copy in side_y[h]:
            copy.wait()
        if h == 0:
            for copy in side_z:
                copy.wait()
        lo, hi = h * part, (h + 1) * part
        for c in range(4):
            more = dot(beside[h], halo_state[h, c])
            grad[c, lo:hi] += more[:part]
            grad[c, cells + lo : cells + hi] += more[part:]
        lax.fori_loop(lo // 16, hi // 16, advance, 0)
        f1 = split(flux[1, lo:hi])
        code, top = encode(dot(pick[...], f1[0]) + dot(pick[...], f1[1]))
        code_f[h] = code.astype(jnp.bfloat16)
        top_f[h] = top
        f_side.append(
            side_f(h, code_f, code_halo_f)
            + [
                send(
                    top_f.at[h], top_halo_f.at[h, w], t_send.at[2 * h + w], t_recv.at[2 * h + w],
                    (up_y, down_y)[w],
                )
                for w in range(2)
            ]
        )
        if h == 0:
            f_low = low_f()
    f_top = high_f()
    outgoing = [
        pltpu.make_async_copy(heat_next, heat_out, out_sem.at[0]),
    ]
    for copy in outgoing:
        copy.start()

    f0 = split(flux[0])
    f1 = split(flux[1])
    f2 = split(flux[2])
    div[...] = (
        dot(f0[0], along_x[...]) + dot(f0[1], along_x[...])
        + dot(own[0:cells], f1[0]) + dot(own[0:cells], f1[1])
        + dot(own[cells:], f2[0]) + dot(own[cells:], f2[1])
    )
    def spread(buffer, h):
        lanes = slice(h * part, (h + 1) * part)
        if rows2 % 8 == 0:
            buffer[h] = line[:, lanes].reshape(owners, rows2, part).astype(buffer.dtype)
        else:
            for k in range(owners):
                buffer[h, k] = line[k * rows2 : (k + 1) * rows2, lanes].astype(buffer.dtype)

    def gather(buffer, h):
        if rows2 % 8 == 0:
            return buffer.reshape(owners * rows2, part)
        lanes = slice(h * part, (h + 1) * part)
        for k in range(owners):
            line[k * rows2 : (k + 1) * rows2, lanes] = buffer[k]
        return line[:, lanes]

    def exchange(source, target, send_sem, recv_sem, h, shared=False):
        def begin(oy, oz):
            src = source.at[h, 0] if shared else source.at[h, oy * gz + oz]
            pltpu.make_async_remote_copy(
                src_ref=src, dst_ref=target.at[h, me],
                send_sem=send_sem.at[h], recv_sem=recv_sem.at[h],
                device_id=(oy, oz), device_id_type=mesh_ids,
            ).start()

        to_all(begin)
        target[h, me] = source[h, 0] if shared else source[h, me]

        def done():
            got = target.at[h, 1:owners]
            sent = got if shared else source.at[h, 1:owners]
            pltpu.make_async_copy(got, got, recv_sem.at[h]).wait()
            pltpu.make_async_copy(sent, sent, send_sem.at[h]).wait()

        return done

    def share(source, target, send_sem, recv_sem, h):
        return exchange(source, target, send_sem, recv_sem, h, True)

    pending = []
    for h in range(parts):
        for copy in f_side[h]:
            copy.wait()
        if h == 0:
            f_top.wait()
        if h == last:
            f_low.wait()
        lo, hi = h * part, (h + 1) * part
        for w in range(2):
            rows = slice(w * ye, (w + 1) * ye)
            halo_f[h, rows] = decode(code_halo_f[h, rows], top_halo_f[h, w])
        e = split(halo_f[h])
        d = split((div[lo:hi] + dot(beside_sum[h], e[0]) + dot(beside_sum[h], e[1])) * sixtieth)
        code, top = encode(dot3((big[0], big[1]), d, 1, 1))
        line[:, lo:hi] = code
        top_line[h, 0] = top
        spread(there, h)
        pending.append(exchange(there, here, a_send, a_recv, h))
        pending.append(share(top_line, tops, u_send, u_recv, h))

    half = lx // 2
    halved = []
    for h in range(parts):
        pending[2 * h]()
        pending[2 * h + 1]()
        block = gather(decode(here[h], tops[h]), h)
        halved.append(dot3((big[4], big[5]), split(block)))
    out = jnp.concatenate(halved, axis=1)
    re, im = out[:half], out[half:]
    tr, ti = plane[0], plane[1]
    both = jnp.concatenate([re * tr - im * ti, re * ti + im * tr], axis=1)
    out = dot3(split(both), (big[8], big[9]))
    re, im = out[:, :cells] * factor[...], out[:, cells:] * factor[...]
    both = jnp.concatenate([re, im], axis=1)
    out = dot3(split(both), (big[10], big[11]))
    re, im = out[:, :cells], out[:, cells:]
    both = jnp.concatenate([re * tr + im * ti, im * tr - re * ti], axis=0)
    both = split(both)
    pending = []
    for h in range(parts):
        lanes = slice(h * part, (h + 1) * part)
        line[:, lanes] = dot3((big[6], big[7]), [b[:, lanes] for b in both])
        spread(there2, h)
        pending.append(exchange(there2, here2, b_send, b_recv, h))
    side_p, low_p, top_p = borders(press, edge_p, halo_p, p_send, p_recv)
    p_side = []
    for h in range(parts):
        pending[h]()
        lo, hi = h * part, (h + 1) * part
        press[lo:hi] = dot3(split(gather(here2[h], h)), (big[2], big[3]), 0, 0)
        p = split(press[lo:hi], 3)
        edge_p[h] = dot(pick[...], p[0]) + dot(pick[...], p[1]) + dot(pick[...], p[2])
        p_side.append(side_p(h))
        if h == 0:
            p_low = low_p()
    p_top = top_p()
    p = split(press[...], 3)
    grad[0] = dot(own[...], p[0]) + dot(own[...], p[1]) + dot(own[...], p[2])
    grad_x[0] = dot(p[0], along_x[...]) + dot(p[1], along_x[...]) + dot(p[2], along_x[...])

    def project(i, carry):
        rows = pl.ds(pl.multiple_of(i * 8, 8), 8)
        rows_z = pl.ds(pl.multiple_of(cells + i * 8, 8), 8)
        push = [
            grad_x[0, rows, :] * sixtieth, grad[0, rows, :] * sixtieth, grad[0, rows_z, :] * sixtieth
        ]
        for c in range(3):
            flux[c, rows, :] = prov[c, rows, :] - (
                metric[c, 0] * push[0] + metric[c, 1] * push[1] + metric[c, 2] * push[2]
            )
        return carry

    for h in range(parts):
        for copy in p_side[h]:
            copy.wait()
        if h == 0:
            p_top.wait()
        if h == last:
            p_low.wait()
        lo, hi = h * part, (h + 1) * part
        e = split(halo_p[h], 3)
        more = dot(beside[h], e[0]) + dot(beside[h], e[1]) + dot(beside[h], e[2])
        grad[0, lo:hi] += more[:part]
        grad[0, cells + lo : cells + hi] += more[part:]
        lax.fori_loop(lo // 8, hi // 8, project, 0)
        copy = pltpu.make_async_copy(
            flux.at[:, lo:hi], motion_out.at[:, lo:hi], out_sem.at[1 + h]
        )
        copy.start()
        outgoing.append(copy)

    for copy in outgoing:
        copy.wait()


def hand_over(motion, heat, motion_next, heat_next):
    motion_next[...] = motion[...]
    heat_next[...] = heat[...]


def shards(flow_state, metric, deformation):
    gy, gz = lax.axis_size("gy"), lax.axis_size("gz")
    owners = gy * gz
    _, ez, ey, lx = flow_state.shape
    cells = ez * ey
    m = lx // 2 // owners
    own, beside, pick, along_x = stencil_tables(ez, ey, lx)
    cos_x, sin_x, weight = x_tables(lx)
    ahead = by_owner(cos_x, sin_x, owners)
    back = by_owner(cos_x * weight, sin_x * weight, owners)
    twist, kron, block, ky, kz, edge = plane_tables(gy, gz, ey, ez)
    eye = np.eye(m)
    br, bi = np.cos(block), np.sin(block)
    pair = np.stack([np.stack([br, -bi], 1), np.stack([bi, br], 1)], 0)
    across = np.einsum("atsb,mn->atmsbn", pair.transpose(0, 1, 3, 2), eye)
    across = across.reshape(lx, lx)
    wr, wi = np.cos(kron), np.sin(kron)
    within = np.block([[wr, wi], [-wi, wr]])
    big = np.stack(
        halves(ahead) + halves(back) + halves(across) + halves(across.T)
        + halves(within) + halves(within.T)
    )
    plane = np.repeat(
        np.stack([np.cos(twist), np.sin(twist), ky, kz, edge.astype(np.float64)]), m, axis=1
    ).astype(np.float32)
    bf = jnp.bfloat16
    f32 = jnp.float32
    vmem = pl.BlockSpec(memory_space=pltpu.VMEM)
    smem = pl.BlockSpec(memory_space=pltpu.SMEM)
    hbm = pl.BlockSpec(memory_space=pl.ANY)
    zc = ez // parts
    wide = 6 * zc + 4 * ey
    part = zc * ey
    dma = pltpu.SemaphoreType.DMA
    motion, heat = pl.pallas_call(
        lambda *refs: kernel((gy, gz, ez, ey, lx), *refs),
        out_shape=(
            jax.ShapeDtypeStruct((3, cells, lx), f32), jax.ShapeDtypeStruct((cells, lx), f32),
        ),
        in_specs=[smem, smem] + [hbm] * 4 + [vmem] + [hbm] * 3,
        out_specs=(hbm,) * 2,
        scratch_shapes=[
            pltpu.VMEM((4, cells, lx), bf),
            pltpu.VMEM(own.shape, bf),
            pltpu.VMEM(beside.shape, bf),
            pltpu.VMEM((parts, part, wide), bf),
            pltpu.VMEM((lx, lx), bf),
            pltpu.VMEM((cells, lx), f32),
            pltpu.VMEM(big.shape, bf),
            pltpu.VMEM(plane.shape, f32),
            pltpu.VMEM((parts, 2, 4, 3 * zc, lx), bf),
            pltpu.VMEM((parts, 4, wide, lx), bf),
            pltpu.VMEM((4, 2 * cells, lx), f32),
            pltpu.VMEM((4, cells, lx), f32),
            pltpu.VMEM((3, cells, lx), f32),
            pltpu.VMEM((3, cells, lx), f32),
            pltpu.VMEM((parts, 6 * zc, lx), f32),
            pltpu.VMEM((parts, wide, lx), f32),
            pltpu.VMEM((cells, lx), f32),
            pltpu.VMEM((parts, 6 * zc, lx), bf),
            pltpu.VMEM((parts, 6 * zc, lx), bf),
            pltpu.VMEM((parts, 1, lx), f32),
            pltpu.VMEM((parts, 2, 1, lx), f32),
            pltpu.VMEM((parts, owners, 1, part), f32),
            pltpu.VMEM((parts, 1, 1, part), f32),
            pltpu.VMEM((parts, 6 * zc, lx), f32),
            pltpu.VMEM((parts, wide, lx), f32),
            pltpu.VMEM((cells, lx), f32),
            pltpu.VMEM((lx, cells), f32),
        ]
        + [pltpu.VMEM((parts, owners, 2 * m, part), bf)] * 2
        + [pltpu.VMEM((parts, owners, 2 * m, part), f32)] * 2
        + [pltpu.VMEM((lx // 2, cells), f32)]
        + [dma((7,)), dma((1 + parts,))] + [dma((2 * parts,))] * 2 + [dma((parts,))] * 2 + [dma((2 * parts + 2,))] * 6 + [dma((parts,))] * 4,
        compiler_params=pltpu.CompilerParams(
            collective_id=0, has_side_effects=True, vmem_limit_bytes=56 * 2**20
        ),
        cost_estimate=pl.CostEstimate(
            flops=4 * 10**9, bytes_accessed=12 * 2**20, transcendentals=0
        ),
        name="substep",
    )(
        metric, deformation, flow_state.reshape(4, cells, lx),
        jnp.asarray(own, bf), jnp.asarray(beside, bf),
        jnp.asarray(beside[:, :part] + beside[:, part:], bf), jnp.asarray(pick, bf),
        jnp.asarray(along_x, bf), jnp.asarray(big), jnp.asarray(plane),
    )
    steps = 4
    block = cells // steps
    specs = (
        pl.BlockSpec((3, block, lx), lambda i: (0, i, 0)), pl.BlockSpec((block, lx), lambda i: (i, 0))
    )
    motion, heat_next = pl.pallas_call(
        hand_over,
        grid=(steps,),
        out_shape=(
            jax.ShapeDtypeStruct((3, cells, lx), f32), jax.ShapeDtypeStruct((cells, lx), f32)
        ),
        in_specs=list(specs),
        out_specs=specs,
        compiler_params=pltpu.CompilerParams(vmem_limit_bytes=60 * 2**20),
        name="hand_over",
    )(motion, heat)
    return motion.reshape(3, ez, ey, lx), heat_next.reshape(ez, ey, lx)

def solution(mesh):
    placed = (P(None, "gz", "gy", None), P(), P())
    return jax.shard_map(
        shards,
        mesh=mesh,
        in_specs=placed,
        out_specs=(P(None, "gz", "gy", None), P("gz", "gy", None)),
        check_vma=False,
    )
```
